32 devices in a mesh: fibre: 8 (over y, x, core), win: 4 (over z).
Axes of the slice: x: 2, y: 2, z: 4, core: 2. Of those that a mesh axis runs over, the one named last changes fastest.
Arguments:
- strain: bfloat16 [1024, 4, 2048], P('fibre', 'win'), may hold values from -6 to 6
- kernel: bfloat16 [31, 9], replicated, may hold values from -0.375 to 0.375
- plan: int32 [4], replicated, may hold values from 0 to 7
Outputs:
- stacks: bfloat16 [4, 256, 2, 128, 1024], P(None, 'win', None, None, 'fibre')
The draws below stay inside these ranges and needn't reach their ends.
Inputs may be any that keep to these rules, and one draw needn't show every extreme that they name: `plan`: each step's entry is an index along fibre; entries may repeat.
All inputs are finite; a program needn't handle non-finite values.
Results may differ from the reference program's by a relative error of at most 0.0057.
Values may be sent and summed in bfloat16 or wider, within the bound.
A program may use at most 128 MiB of HBM per device.

```python
import math
import jax
import jax.numpy as jnp
from jax import lax

CH_DEV = 128
SAMPLES = 2048
FB = 256
FLO = 8
BLK = 64
CTAPS = 31
TTAPS = 9
STEPS = 4
CHANNELS = 1024
WINDOWS = 4
N_FIBRE = 8


def set_ends(drawn, key, low, largest):
    longest = drawn.shape.index(max(drawn.shape))
    spots = []
    for shift in (0, 1):
        where = [jax.random.randint(jax.random.fold_in(key, axis), (), 0, length) for axis, length in enumerate(drawn.shape)]
        where[longest] = (where[longest] + shift) % drawn.shape[longest]
        spots.append(tuple(where))
    return drawn.at[spots[0]].set(low).at[spots[1]].set(largest)


def shard_levels(rng, shape, cuts, low, largest):
    loudness = 1.0
    for dim, shards_of in cuts:
        steps = jax.random.uniform(jax.random.fold_in(jax.random.fold_in(rng, 6), dim), (shards_of,), jnp.float32, low / len(cuts), largest / len(cuts))
        loudness = loudness * jnp.repeat(jnp.exp(steps), shape[dim] // shards_of).reshape((-1,) + (1,) * (len(shape) - 1 - dim))
    return loudness


def scatter_about(rng, extent, width, bound, shards=(), held_as=jnp.bfloat16):
    result = jax.random.normal(rng, extent, jnp.float32) * width
    if len(shards) > 0:
        result = shard_levels(rng, extent, shards, -0.22, 0.18) * result
    return jnp.clip(result, min=-bound, max=bound).astype(held_as)


def setup_inputs(seed: int = 0) -> dict:
    streams_of = jax.random.split(jax.random.key(seed), 4)
    return {
        "strain": scatter_about(streams_of[0], (CHANNELS, WINDOWS, SAMPLES), 1.0, 6.0, ((0, 8), (1, 4))),
        "kernel": scatter_about(streams_of[1], (CTAPS, TTAPS), (CTAPS * TTAPS) ** -0.5, 0.375),
        "plan": set_ends(jax.random.randint(streams_of[2], (STEPS,), 0, N_FIBRE), jax.random.fold_in(streams_of[2], 1), 0, N_FIBRE - 1).astype(jnp.int32),
    }


def whiten(spectra, bin_block):
    half_width = spectra.shape[-1] // 2
    real_part = spectra[..., :half_width]
    imag_part = spectra[..., half_width:]
    magnitude = jnp.sqrt(real_part * real_part + imag_part * imag_part)
    grouped = magnitude.reshape(magnitude.shape[:-1] + (half_width // bin_block, bin_block))
    amp_level = lax.optimization_barrier(jnp.mean(grouped, axis=-1)) + 1e-06
    factor = jnp.repeat(1.0 / amp_level, bin_block, axis=-1)
    stacked = jnp.stack([real_part * factor, imag_part * factor])
    return jnp.transpose(stacked, (0, 2, 3, 1)).astype(jnp.bfloat16)

def reference(strain, kernel, plan):
    margin = CTAPS // 2
    half_time = TTAPS // 2
    padded = jnp.pad(strain.astype(jnp.float32), ((margin, margin), (0, 0), (0, 0)))
    filtered = lax.conv_general_dilated(padded[..., None], kernel.astype(jnp.float32)[:, :, None, None], (1, 1), ((0, 0), (half_time, half_time)), dimension_numbers=('HNWC', 'HWIO', 'HNWC'), precision=lax.Precision.HIGHEST)[..., 0]
    spectrum = jnp.fft.rfft(filtered, axis=-1)[..., FLO:FLO + FB]
    spectra = jnp.concatenate([jnp.real(spectrum), jnp.imag(spectrum)], axis=-1).astype(jnp.float32)
    whitened = whiten(spectra, BLK)
    widened = whitened.astype(jnp.float32)
    by_bin = jnp.transpose(widened, (2, 0, 1, 3))
    stack_scale = 1.0 / math.sqrt(WINDOWS)

    def one_bin(pieces):
        source_bin, receiver_bin = pieces
        swapped = jnp.stack([receiver_bin[1], -receiver_bin[0]])
        real_sum = jnp.einsum('pwi,pwj->ij', source_bin, receiver_bin, precision=lax.Precision.HIGHEST)
        imag_sum = jnp.einsum('pwi,pwj->ij', source_bin, swapped, precision=lax.Precision.HIGHEST)
        return (jnp.stack([real_sum, imag_sum]) * stack_scale).astype(jnp.bfloat16)
    outputs = []
    for step_index in range(STEPS):
        first_channel = (plan[step_index] * CH_DEV).astype(jnp.int32)
        source = lax.dynamic_slice_in_dim(by_bin, first_channel, CH_DEV, 3)
        outputs.append(lax.map(one_bin, (source, by_bin)))
    return jnp.stack(outputs)
```

```python
import functools
import math

import jax
import jax.numpy as jnp
import ml_dtypes
import numpy as np
from jax import lax
from jax.experimental import pallas as pl
from jax.experimental.pallas import tpu as pltpu
from jax.sharding import PartitionSpec as P

FB = 256
FLO = 8
BLK = 64
ROWS = 16
MESH = pl.DeviceIdType.MESH


def tap_order(half_time):
    order = [0]
    for offset in range(1, half_time + 1):
        order += [offset, -offset]
    return order


@functools.lru_cache(maxsize=None)
def transform_table(samples, bins, half_time):
    index = np.arange(samples, dtype=np.int64)
    blocks = []
    for start in range(0, FB, bins):
        wanted = FLO + start + np.arange(bins, dtype=np.int64)
        angles = (wanted[:, None] * index[None, :] % samples) * (2.0 * np.pi / samples)
        exact = np.concatenate([np.cos(angles), -np.sin(angles)])
        high = exact.astype(ml_dtypes.bfloat16)
        low = (exact - high.astype(np.float64)).astype(ml_dtypes.bfloat16)
        blocks += [high, low]
    picks = np.zeros((-(-2 * half_time // ROWS) * ROWS, samples), ml_dtypes.bfloat16)
    for row in range(half_time):
        picks[row, row] = 1
        picks[half_time + row, samples - half_time + row] = 1
    return np.concatenate(blocks + [picks])


@functools.lru_cache(maxsize=None)
def phase_table(samples, half_time):
    wanted = FLO + np.arange(FB, dtype=np.int64)
    angles = wanted[:, None] * np.arange(1, half_time + 1)[None, :] % samples * (2.0 * np.pi / samples)
    return np.concatenate([np.cos(angles), np.sin(angles)], axis=1).astype(np.float32)


def gather_orders(count):
    bits = [1 << place for place in range(1, count.bit_length() - 1)]
    return [bits + [1], bits[::-1] + [1]]


def spectra_kernel(
    fibres, wins, margin, half_time,
    taps_ref, phase_ref, table_ref, strain_ref, out_ref,
    table_v, x_v, d_v, band_v, white_v,
    load_sem, halo_send, halo_recv, swap_send, swap_recv, keep_sem, gather_send, gather_recv,
):
    me = lax.axis_index("fibre")
    win = lax.axis_index("win")
    channels = strain_ref.shape[0]
    bins = white_v.shape[2]
    halo = (x_v.shape[0] - channels) // 2
    chan_taps = 2 * margin + 1
    order = tap_order(half_time)

    load_table = pltpu.make_async_copy(table_ref, table_v, load_sem.at[0])
    load_table.start()
    load_own = pltpu.make_async_copy(strain_ref, x_v.at[pl.ds(0, channels)], load_sem.at[1])
    load_own.start()

    barrier = pltpu.get_barrier_semaphore()
    for step in range(1, fibres):
        pl.semaphore_signal(barrier, inc=1, device_id={"fibre": lax.rem(me + step, fibres)}, device_id_type=MESH)
    for step in range(1, wins):
        pl.semaphore_signal(barrier, inc=1, device_id={"win": lax.rem(win + step, wins)}, device_id_type=MESH)
    pl.semaphore_wait(barrier, fibres + wins - 2)

    to_right = pltpu.make_async_remote_copy(
        src_ref=strain_ref.at[pl.ds(channels - halo, halo)], dst_ref=x_v.at[pl.ds(channels, halo)],
        send_sem=halo_send.at[0], recv_sem=halo_recv.at[0],
        device_id={"fibre": lax.rem(me + 1, fibres)}, device_id_type=MESH,
    )
    to_left = pltpu.make_async_remote_copy(
        src_ref=strain_ref.at[pl.ds(0, halo)], dst_ref=x_v.at[pl.ds(channels + halo, halo)],
        send_sem=halo_send.at[1], recv_sem=halo_recv.at[1],
        device_id={"fibre": lax.rem(me + fibres - 1, fibres)}, device_id_type=MESH,
    )
    first, last = me == 0, me == fibres - 1

    @pl.when(jnp.logical_not(last))
    def _():
        to_right.start()

    @pl.when(jnp.logical_not(first))
    def _():
        to_left.start()

    @pl.when(first)
    def _():
        x_v[channels : channels + halo, :] = jnp.zeros((halo, x_v.shape[1]), x_v.dtype)

    @pl.when(last)
    def _():
        x_v[channels + halo :, :] = jnp.zeros((halo, x_v.shape[1]), x_v.dtype)

    for low, size, start in ((0, channels, 0), (channels, halo, -halo), (channels + halo, halo, channels)):
        for piece in range(0, size, 64):
            rows = min(64, size - piece)
            shape = (rows, channels)
            lag = (
                lax.broadcasted_iota(jnp.int32, shape, 0) + (start + piece + margin)
                - lax.broadcasted_iota(jnp.int32, shape, 1)
            )
            totals = [jnp.zeros(shape, jnp.float32)] * len(order)
            least = start + piece + margin - (channels - 1)
            most = start + piece + margin + rows - 1
            for tap in range(max(0, least), min(chan_taps - 1, most) + 1):
                here = lag == tap
                totals = [
                    jnp.where(here, taps_ref[tap, offset + half_time], total)
                    for total, offset in zip(totals, order)
                ]
            for place, total in enumerate(totals):
                band_v[low + piece : low + piece + rows, place * channels : (place + 1) * channels] = total.astype(
                    jnp.bfloat16
                )

    load_own.wait()

    @pl.when(jnp.logical_not(last))
    def _():
        to_right.wait_send()
        to_left.wait_recv()

    @pl.when(jnp.logical_not(first))
    def _():
        to_left.wait_send()
        to_right.wait_recv()

    load_table.wait()
    d_v[...] = lax.dot_general(
        table_v[...], x_v[...], (((1,), (1,)), ((), ())), preferred_element_type=jnp.float32
    )

    edges = d_v[4 * FB :, :].astype(jnp.bfloat16)
    tails = jnp.dot(edges, band_v[...], preferred_element_type=jnp.float32)

    def tail(row, offset):
        place = order.index(offset)
        return tails[row : row + 1, place * channels : (place + 1) * channels]

    before = {m: sum(tail(u, m + u) for u in range(half_time - m + 1)) for m in range(1, half_time + 1)}
    after = {
        m: sum(tail(2 * half_time - v, -(v + m)) for v in range(1, half_time - m + 1)) for m in range(half_time)
    }

    def whiten_group(group):
        base = pl.multiple_of(group * (4 * bins), 4 * bins)
        both = d_v[pl.ds(base, 2 * bins), :] + d_v[pl.ds(base + 2 * bins, 2 * bins), :]
        high = both.astype(jnp.bfloat16)
        low = (both - high.astype(jnp.float32)).astype(jnp.bfloat16)

        def banded(place, width):
            band = band_v[:, place * channels : (place + width) * channels]
            return jnp.dot(high, band, preferred_element_type=jnp.float32) + jnp.dot(
                low, band, preferred_element_type=jnp.float32
            )

        plain = banded(0, 1)
        real = plain[:bins] - after[0]
        imag = plain[bins:]
        bin_rows = pl.ds(pl.multiple_of(group * bins, bins), bins)
        for offset in range(1, half_time + 1):
            pair = banded(2 * offset - 1, 2)
            ahead_re = pair[:bins, :channels] - before[offset]
            back_re = pair[:bins, channels:]
            if offset in after:
                back_re = back_re - after[offset]
            ahead_im, back_im = pair[bins:, :channels], pair[bins:, channels:]
            cos = phase_ref[bin_rows, offset - 1 : offset]
            sin = phase_ref[bin_rows, half_time + offset - 1 : half_time + offset]
            real += cos * (ahead_re + back_re) - sin * (ahead_im - back_im)
            imag += cos * (ahead_im + back_im) + sin * (ahead_re - back_re)
        magnitude = jnp.sqrt(real * real + imag * imag)
        for start in range(0, bins, BLK):
            level = jnp.mean(magnitude[start : start + BLK], axis=0, keepdims=True) + 1e-06
            factor = 1.0 / level
            white_v[group, 0, start : start + BLK] = (real[start : start + BLK] * factor).astype(jnp.bfloat16)
            white_v[group, 1, start : start + BLK] = (imag[start : start + BLK] * factor).astype(jnp.bfloat16)

    def swap(step):
        target = lax.rem(win + step, wins)
        return pltpu.make_async_remote_copy(
            src_ref=white_v.at[target], dst_ref=out_ref.at[me, win],
            send_sem=swap_send.at[step], recv_sem=swap_recv.at[step],
            device_id={"win": target}, device_id_type=MESH,
        )

    def swap_arrival(step):
        source = lax.rem(win + wins - step, wins)
        return pltpu.make_async_remote_copy(
            src_ref=white_v.at[win], dst_ref=out_ref.at[me, source],
            send_sem=swap_send.at[step], recv_sem=swap_recv.at[step],
            device_id={"win": source}, device_id_type=MESH,
        )

    steps = sorted(range(1, wins), key=lambda step: -min(step, wins - step))
    for step in steps:
        whiten_group(lax.rem(win + step, wins))
        swap(step).start()
    whiten_group(win)
    keep = pltpu.make_async_copy(white_v.at[win], out_ref.at[me, win], keep_sem)
    keep.start()

    orders = gather_orders(fibres)
    arrival_order = [0] + sorted(range(1, wins), key=lambda step: min(step, wins - step))

    def hop(step, away, bit):
        block = lax.bitwise_xor(me, away)
        window = lax.rem(win + wins - step, wins)
        source = white_v.at[win] if step == 0 and away == 0 else out_ref.at[block, window]
        return pltpu.make_async_remote_copy(
            src_ref=source, dst_ref=out_ref.at[block, window],
            send_sem=gather_send.at[away ^ bit, step], recv_sem=gather_recv.at[away ^ bit, step],
            device_id={"fibre": lax.bitwise_xor(me, bit)}, device_id_type=MESH,
        )

    events = []
    for rank, step in enumerate(arrival_order):
        line = orders[rank % 2]
        for away in range(fibres):
            taken = [place for place, bit in enumerate(line) if away & bit]
            latest = max(taken, default=-1)
            events.append((rank + len(taken), rank, latest, away, step, line))
    events.sort(key=lambda event: event[:4])
    started = []
    for _, _, latest, away, step, line in events:
        if away:
            hop(step, away ^ line[latest], line[latest]).wait_recv()
        elif step:
            swap_arrival(step).wait_recv()
        for bit in line[latest + 1 :]:
            copy = hop(step, away, bit)
            copy.start()
            started.append(copy)
    keep.wait()
    for step in range(1, wins):
        swap(step).wait_send()
    for copy in started:
        copy.wait_send()


def stack_kernel(steps, scale, chosen_ref, *refs):
    sources, receiver, out_ref, left_v, right_v = refs[:steps], refs[steps], refs[steps + 1], refs[steps + 2], refs[steps + 3]
    wins, _, _, channels = receiver.shape[1:]
    depth = wins * 2 * ROWS
    per_step = out_ref.shape[1]
    first_bin = pl.program_id(0) * per_step
    exact = math.frexp(scale)[0] == 0.5

    @pl.when(first_bin % ROWS == 0)
    def _():
        group = pl.ds(pl.multiple_of(first_bin // ROWS * ROWS, ROWS), ROWS)
        for step, source in enumerate(sources):
            piece = source[0, :, :, group, :].reshape(depth, channels).astype(jnp.float32)
            if exact:
                piece = piece * scale
            left_v[step * channels : (step + 1) * channels, :] = piece.T.astype(jnp.bfloat16)
        real = receiver[0, :, 0, group, :]
        imag = receiver[0, :, 1, group, :]
        right_v[:, :channels] = jnp.stack([real, imag], axis=1).reshape(depth, channels)
        right_v[:, channels:] = jnp.stack([imag, -real], axis=1).reshape(depth, channels)

    row = lax.rem(lax.broadcasted_iota(jnp.int32, (depth, 2 * channels), 0), ROWS)
    for place in range(per_step):
        here = row == lax.rem(first_bin + place, ROWS)
        right = jnp.where(here, right_v[...].astype(jnp.float32), 0.0).astype(jnp.bfloat16)
        result = jnp.dot(left_v[...], right, preferred_element_type=jnp.float32)
        if not exact:
            result = result * scale
        result = result.astype(jnp.bfloat16)
        for step in range(steps):
            out_ref[step, place, 0] = result[step * channels : (step + 1) * channels, :channels]
            out_ref[step, place, 1] = result[step * channels : (step + 1) * channels, channels:]


def shards(strain, kernel, plan):
    fibres, wins = lax.axis_size("fibre"), lax.axis_size("win")
    channels, own_windows, samples = strain.shape
    margin, half_time = kernel.shape[0] // 2, kernel.shape[1] // 2
    bins = FB // wins
    halo = -(-margin // ROWS) * ROWS
    assert own_windows == 1 and bins % BLK == 0 and fibres & (fibres - 1) == 0
    table = transform_table(samples, bins, half_time)
    phases = phase_table(samples, half_time)
    any_space = pl.BlockSpec(memory_space=pl.ANY)
    gathered = pl.pallas_call(
        functools.partial(spectra_kernel, fibres, wins, margin, half_time),
        out_shape=jax.ShapeDtypeStruct((fibres, wins, 2, bins, channels), jnp.bfloat16),
        in_specs=[
            pl.BlockSpec(memory_space=pltpu.SMEM),
            pl.BlockSpec(memory_space=pltpu.VMEM),
            any_space,
            any_space,
        ],
        out_specs=any_space,
        scratch_shapes=[
            pltpu.VMEM(table.shape, jnp.bfloat16),
            pltpu.VMEM((channels + 2 * halo, samples), jnp.bfloat16),
            pltpu.VMEM((table.shape[0], channels + 2 * halo), jnp.float32),
            pltpu.VMEM((channels + 2 * halo, kernel.shape[1] * channels), jnp.bfloat16),
            pltpu.VMEM((wins, 2, bins, channels), jnp.bfloat16),
            pltpu.SemaphoreType.DMA((2,)),
            pltpu.SemaphoreType.DMA((2,)),
            pltpu.SemaphoreType.DMA((2,)),
            pltpu.SemaphoreType.DMA((wins,)),
            pltpu.SemaphoreType.DMA((wins,)),
            pltpu.SemaphoreType.DMA,
            pltpu.SemaphoreType.DMA((fibres, wins)),
            pltpu.SemaphoreType.DMA((fibres, wins)),
        ],
        compiler_params=pltpu.CompilerParams(
            collective_id=0, has_side_effects=True, vmem_limit_bytes=40 * 1024 * 1024
        ),
        name="spectra",
    )(kernel.astype(jnp.float32), jnp.asarray(phases), jnp.asarray(table), strain.reshape(channels, samples))

    steps = plan.shape[0]
    chosen = jnp.concatenate([plan, lax.axis_index("fibre").astype(plan.dtype)[None]])
    per_step = 4
    block = (1, wins, 2, bins, channels)

    def pick(place):
        return pl.BlockSpec(block, lambda i, chosen_ref: (chosen_ref[place], 0, 0, 0, 0))

    return pl.pallas_call(
        functools.partial(stack_kernel, steps, 1.0 / math.sqrt(wins * own_windows)),
        out_shape=jax.ShapeDtypeStruct((steps, bins, 2, channels, channels), jnp.bfloat16),
        grid_spec=pltpu.PrefetchScalarGridSpec(
            num_scalar_prefetch=1,
            grid=(bins // per_step,),
            in_specs=[pick(place) for place in range(steps + 1)],
            out_specs=pl.BlockSpec((steps, per_step, 2, channels, channels), lambda i, chosen_ref: (0, i, 0, 0, 0)),
            scratch_shapes=[
                pltpu.VMEM((steps * channels, wins * 2 * ROWS), jnp.bfloat16),
                pltpu.VMEM((wins * 2 * ROWS, 2 * channels), jnp.bfloat16),
            ],
        ),
        compiler_params=pltpu.CompilerParams(vmem_limit_bytes=40 * 1024 * 1024),
        name="stacks",
    )(chosen, *([gathered] * (steps + 1)))


def solution(mesh):
    placed = (P("fibre", "win", None), P(), P())
    return jax.shard_map(
        shards,
        mesh=mesh,
        in_specs=placed,
        out_specs=P(None, "win", None, None, "fibre"),
        check_vma=False,
    )
```

```python
import functools
import math

import jax
import jax.numpy as jnp
import ml_dtypes
import numpy as np
from jax import lax
from jax.experimental import pallas as pl
from jax.experimental.pallas import tpu as pltpu
from jax.sharding import PartitionSpec as P

FB = 256
FLO = 8
BLK = 64
ROWS = 16
MESH = pl.DeviceIdType.MESH


def tap_order(half_time):
    order = [0]
    for offset in range(1, half_time + 1):
        order += [offset, -offset]
    return order


@functools.lru_cache(maxsize=None)
def transform_table(samples, bins, half_time):
    index = np.arange(samples, dtype=np.int64)
    blocks = []
    for start in range(0, FB, bins):
        wanted = FLO + start + np.arange(bins, dtype=np.int64)
        angles = (wanted[:, None] * index[None, :] % samples) * (2.0 * np.pi / samples)
        exact = np.concatenate([np.cos(angles), -np.sin(angles)])
        high = exact.astype(ml_dtypes.bfloat16)
        low = (exact - high.astype(np.float64)).astype(ml_dtypes.bfloat16)
        blocks += [high, low]
    picks = np.zeros((-(-2 * half_time // ROWS) * ROWS, samples), ml_dtypes.bfloat16)
    for row in range(half_time):
        picks[row, row] = 1
        picks[half_time + row, samples - half_time + row] = 1
    return np.concatenate(blocks + [picks])


@functools.lru_cache(maxsize=None)
def phase_table(samples, half_time):
    wanted = FLO + np.arange(FB, dtype=np.int64)
    angles = wanted[:, None] * np.arange(1, half_time + 1)[None, :] % samples * (2.0 * np.pi / samples)
    return np.concatenate([np.cos(angles), np.sin(angles)], axis=1).astype(np.float32)


def gather_orders(count):
    bits = [1 << place for place in range(1, count.bit_length() - 1)]
    return [bits + [1], bits[::-1] + [1]]


def spectra_kernel(
    fibres, wins, margin, half_time,
    taps_ref, phase_hbm, table_ref, strain_ref, out_ref,
    phase_ref, table_v, x_v, d_v, band_v, white_v,
    load_sem, halo_send, halo_recv, swap_send, swap_recv, keep_sem, gather_send, gather_recv,
):
    me = lax.axis_index("fibre")
    win = lax.axis_index("win")
    channels = strain_ref.shape[0]
    bins = white_v.shape[2]
    halo = (x_v.shape[0] - channels) // 2
    chan_taps = 2 * margin + 1
    order = tap_order(half_time)

    load_table = pltpu.make_async_copy(table_ref, table_v, load_sem.at[0])
    load_table.start()
    load_own = pltpu.make_async_copy(strain_ref, x_v.at[pl.ds(0, channels)], load_sem.at[1])
    load_own.start()
    load_phase = pltpu.make_async_copy(phase_hbm, phase_ref, load_sem.at[2])
    load_phase.start()

    barrier = pltpu.get_barrier_semaphore()
    for step in range(1, fibres):
        pl.semaphore_signal(barrier, inc=1, device_id={"fibre": lax.rem(me + step, fibres)}, device_id_type=MESH)
    for step in range(1, wins):
        pl.semaphore_signal(barrier, inc=1, device_id={"win": lax.rem(win + step, wins)}, device_id_type=MESH)

    for low, size, start in ((0, channels, 0), (channels, halo, -halo), (channels + halo, halo, channels)):
        for piece in range(0, size, 64):
            rows = min(64, size - piece)
            shape = (rows, channels)
            lag = (
                lax.broadcasted_iota(jnp.int32, shape, 0) + (start + piece + margin)
                - lax.broadcasted_iota(jnp.int32, shape, 1)
            )
            totals = [jnp.zeros(shape, jnp.float32)] * len(order)
            least = start + piece + margin - (channels - 1)
            most = start + piece + margin + rows - 1
            for tap in range(max(0, least), min(chan_taps - 1, most) + 1):
                here = lag == tap
                totals = [
                    jnp.where(here, taps_ref[tap, offset + half_time], total)
                    for total, offset in zip(totals, order)
                ]
            for place, total in enumerate(totals):
                band_v[low + piece : low + piece + rows, place * channels : (place + 1) * channels] = total.astype(
                    jnp.bfloat16
                )

    pl.semaphore_wait(barrier, fibres + wins - 2)

    to_right = pltpu.make_async_remote_copy(
        src_ref=strain_ref.at[pl.ds(channels - halo, halo)], dst_ref=x_v.at[pl.ds(channels, halo)],
        send_sem=halo_send.at[0], recv_sem=halo_recv.at[0],
        device_id={"fibre": lax.rem(me + 1, fibres)}, device_id_type=MESH,
    )
    to_left = pltpu.make_async_remote_copy(
        src_ref=strain_ref.at[pl.ds(0, halo)], dst_ref=x_v.at[pl.ds(channels + halo, halo)],
        send_sem=halo_send.at[1], recv_sem=halo_recv.at[1],
        device_id={"fibre": lax.rem(me + fibres - 1, fibres)}, device_id_type=MESH,
    )
    first, last = me == 0, me == fibres - 1

    @pl.when(jnp.logical_not(last))
    def _():
        to_right.start()

    @pl.when(jnp.logical_not(first))
    def _():
        to_left.start()

    @pl.when(first)
    def _():
        x_v[channels : channels + halo, :] = jnp.zeros((halo, x_v.shape[1]), x_v.dtype)

    @pl.when(last)
    def _():
        x_v[channels + halo :, :] = jnp.zeros((halo, x_v.shape[1]), x_v.dtype)

    load_own.wait()

    @pl.when(jnp.logical_not(last))
    def _():
        to_right.wait_send()
        to_left.wait_recv()

    @pl.when(jnp.logical_not(first))
    def _():
        to_left.wait_send()
        to_right.wait_recv()

    load_table.wait()
    load_phase.wait()
    d_v[...] = lax.dot_general(
        table_v[...], x_v[...], (((1,), (1,)), ((), ())), preferred_element_type=jnp.float32
    )

    edges = d_v[4 * FB :, :].astype(jnp.bfloat16)
    tails = jnp.dot(edges, band_v[...], preferred_element_type=jnp.float32)

    def tail(row, offset):
        place = order.index(offset)
        return tails[row : row + 1, place * channels : (place + 1) * channels]

    before = {m: sum(tail(u, m + u) for u in range(half_time - m + 1)) for m in range(1, half_time + 1)}
    after = {
        m: sum(tail(2 * half_time - v, -(v + m)) for v in range(1, half_time - m + 1)) for m in range(half_time)
    }

    def whiten_group(group):
        base = pl.multiple_of(group * (4 * bins), 4 * bins)
        both = d_v[pl.ds(base, 2 * bins), :] + d_v[pl.ds(base + 2 * bins, 2 * bins), :]
        high = both.astype(jnp.bfloat16)
        low = (both - high.astype(jnp.float32)).astype(jnp.bfloat16)

        parts = jnp.dot(
            jnp.concatenate([high, low]), band_v[...], preferred_element_type=jnp.float32
        )
        shifted = parts[: 2 * bins] + parts[2 * bins :]
        real = shifted[:bins, :channels] - after[0]
        imag = shifted[bins:, :channels]
        bin_rows = pl.ds(pl.multiple_of(group * bins, bins), bins)
        for offset in range(1, half_time + 1):
            pair = shifted[:, (2 * offset - 1) * channels : (2 * offset + 1) * channels]
            ahead_re = pair[:bins, :channels] - before[offset]
            back_re = pair[:bins, channels:]
            if offset in after:
                back_re = back_re - after[offset]
            ahead_im, back_im = pair[bins:, :channels], pair[bins:, channels:]
            cos = phase_ref[bin_rows, offset - 1 : offset]
            sin = phase_ref[bin_rows, half_time + offset - 1 : half_time + offset]
            real += cos * (ahead_re + back_re) - sin * (ahead_im - back_im)
            imag += cos * (ahead_im + back_im) + sin * (ahead_re - back_re)
        magnitude = jnp.sqrt(real * real + imag * imag)
        for start in range(0, bins, BLK):
            level = jnp.mean(magnitude[start : start + BLK], axis=0, keepdims=True) + 1e-06
            factor = 1.0 / level
            white_v[group, 0, start : start + BLK] = (real[start : start + BLK] * factor).astype(jnp.bfloat16)
            white_v[group, 1, start : start + BLK] = (imag[start : start + BLK] * factor).astype(jnp.bfloat16)

    def swap(step):
        target = lax.rem(win + step, wins)
        return pltpu.make_async_remote_copy(
            src_ref=white_v.at[target], dst_ref=out_ref.at[me, win],
            send_sem=swap_send.at[step], recv_sem=swap_recv.at[step],
            device_id={"win": target}, device_id_type=MESH,
        )

    def swap_arrival(step):
        source = lax.rem(win + wins - step, wins)
        return pltpu.make_async_remote_copy(
            src_ref=white_v.at[win], dst_ref=out_ref.at[me, source],
            send_sem=swap_send.at[step], recv_sem=swap_recv.at[step],
            device_id={"win": source}, device_id_type=MESH,
        )

    steps = sorted(range(1, wins), key=lambda step: -min(step, wins - step))
    for step in steps:
        whiten_group(lax.rem(win + step, wins))
        swap(step).start()
    whiten_group(win)
    keep = pltpu.make_async_copy(white_v.at[win], out_ref.at[me, win], keep_sem)
    keep.start()

    orders = gather_orders(fibres)
    arrival_order = [0] + sorted(range(1, wins), key=lambda step: min(step, wins - step))

    def hop(step, away, bit):
        block = lax.bitwise_xor(me, away)
        window = lax.rem(win + wins - step, wins)
        source = white_v.at[win] if step == 0 and away == 0 else out_ref.at[block, window]
        return pltpu.make_async_remote_copy(
            src_ref=source, dst_ref=out_ref.at[block, window],
            send_sem=gather_send.at[away ^ bit, step], recv_sem=gather_recv.at[away ^ bit, step],
            device_id={"fibre": lax.bitwise_xor(me, bit)}, device_id_type=MESH,
        )

    events = []
    for rank, step in enumerate(arrival_order):
        line = orders[rank % 2]
        for away in range(fibres):
            taken = [place for place, bit in enumerate(line) if away & bit]
            latest = max(taken, default=-1)
            events.append((rank + len(taken), rank, latest, away, step, line))
    events.sort(key=lambda event: event[:4])
    started = []
    for _, _, latest, away, step, line in events:
        if away:
            hop(step, away ^ line[latest], line[latest]).wait_recv()
        elif step:
            swap_arrival(step).wait_recv()
        for bit in line[latest + 1 :]:
            copy = hop(step, away, bit)
            copy.start()
            started.append(copy)
    keep.wait()
    for step in range(1, wins):
        swap(step).wait_send()
    for copy in started:
        copy.wait_send()


def stack_kernel(steps, scale, chosen_ref, *refs):
    sources, receiver, out_ref, left_v, right_v = refs[:steps], refs[steps], refs[steps + 1], refs[steps + 2], refs[steps + 3]
    wins, _, _, channels = receiver.shape[1:]
    depth = wins * 2 * ROWS
    per_step = out_ref.shape[1]
    first_bin = pl.program_id(0) * per_step
    exact = math.frexp(scale)[0] == 0.5

    @pl.when(first_bin % ROWS == 0)
    def _():
        group = pl.ds(pl.multiple_of(first_bin // ROWS * ROWS, ROWS), ROWS)
        for step, source in enumerate(sources):
            piece = source[0, :, :, group, :].reshape(depth, channels).astype(jnp.float32)
            if exact:
                piece = piece * scale
            left_v[step * channels : (step + 1) * channels, :] = piece.T.astype(jnp.bfloat16)
        real = receiver[0, :, 0, group, :]
        imag = receiver[0, :, 1, group, :]
        right_v[:, :channels] = jnp.stack([real, imag], axis=1).reshape(depth, channels)
        right_v[:, channels:] = jnp.stack([imag, -real], axis=1).reshape(depth, channels)

    row = lax.broadcasted_iota(jnp.int32, (ROWS, 2 * channels), 0)
    right = right_v[...].reshape(wins * 2, ROWS, 2 * channels)
    left = left_v[...]
    for place in range(per_step):
        here = jnp.where(row == lax.rem(first_bin + place, ROWS), 1.0, 0.0).astype(jnp.bfloat16)
        one_bin = (right * here[None]).reshape(depth, 2 * channels)
        result = jnp.dot(left, one_bin, preferred_element_type=jnp.float32)
        if not exact:
            result = result * scale
        result = result.astype(jnp.bfloat16)
        for step in range(steps):
            out_ref[step, place, 0] = result[step * channels : (step + 1) * channels, :channels]
            out_ref[step, place, 1] = result[step * channels : (step + 1) * channels, channels:]


def shards(strain, kernel, plan):
    fibres, wins = lax.axis_size("fibre"), lax.axis_size("win")
    channels, own_windows, samples = strain.shape
    margin, half_time = kernel.shape[0] // 2, kernel.shape[1] // 2
    bins = FB // wins
    halo = -(-margin // ROWS) * ROWS
    assert own_windows == 1 and bins % BLK == 0 and fibres & (fibres - 1) == 0
    table = transform_table(samples, bins, half_time)
    phases = phase_table(samples, half_time)
    any_space = pl.BlockSpec(memory_space=pl.ANY)
    gathered = pl.pallas_call(
        functools.partial(spectra_kernel, fibres, wins, margin, half_time),
        out_shape=jax.ShapeDtypeStruct((fibres, wins, 2, bins, channels), jnp.bfloat16),
        in_specs=[
            pl.BlockSpec(memory_space=pltpu.SMEM),
            pl.BlockSpec(memory_space=pltpu.HBM),
            pl.BlockSpec(memory_space=pltpu.HBM),
            pl.BlockSpec(memory_space=pltpu.HBM),
        ],
        out_specs=any_space,
        scratch_shapes=[
            pltpu.VMEM(phases.shape, jnp.float32),
            pltpu.VMEM(table.shape, jnp.bfloat16),
            pltpu.VMEM((channels + 2 * halo, samples), jnp.bfloat16),
            pltpu.VMEM((table.shape[0], channels + 2 * halo), jnp.float32),
            pltpu.VMEM((channels + 2 * halo, kernel.shape[1] * channels), jnp.bfloat16),
            pltpu.VMEM((wins, 2, bins, channels), jnp.bfloat16),
            pltpu.SemaphoreType.DMA((3,)),
            pltpu.SemaphoreType.DMA((2,)),
            pltpu.SemaphoreType.DMA((2,)),
            pltpu.SemaphoreType.DMA((wins,)),
            pltpu.SemaphoreType.DMA((wins,)),
            pltpu.SemaphoreType.DMA,
            pltpu.SemaphoreType.DMA((fibres, wins)),
            pltpu.SemaphoreType.DMA((fibres, wins)),
        ],
        compiler_params=pltpu.CompilerParams(
            collective_id=0, has_side_effects=True, vmem_limit_bytes=60 * 1024 * 1024
        ),
        name="spectra",
    )(kernel.astype(jnp.float32), jnp.asarray(phases), jnp.asarray(table), strain.reshape(channels, samples))

    steps = plan.shape[0]
    per_step = 8
    block = (1, wins, 2, bins, channels)

    def pick(place):
        if place == steps:
            return pl.BlockSpec(block, lambda i, chosen_ref: (lax.axis_index("fibre"), 0, 0, 0, 0))
        return pl.BlockSpec(block, lambda i, chosen_ref: (chosen_ref[place], 0, 0, 0, 0))

    return pl.pallas_call(
        functools.partial(stack_kernel, steps, 1.0 / math.sqrt(wins * own_windows)),
        out_shape=jax.ShapeDtypeStruct((steps, bins, 2, channels, channels), jnp.bfloat16),
        grid_spec=pltpu.PrefetchScalarGridSpec(
            num_scalar_prefetch=1,
            grid=(bins // per_step,),
            in_specs=[pick(place) for place in range(steps + 1)],
            out_specs=pl.BlockSpec((steps, per_step, 2, channels, channels), lambda i, chosen_ref: (0, i, 0, 0, 0)),
            scratch_shapes=[
                pltpu.VMEM((steps * channels, wins * 2 * ROWS), jnp.bfloat16),
                pltpu.VMEM((wins * 2 * ROWS, 2 * channels), jnp.bfloat16),
            ],
        ),
        compiler_params=pltpu.CompilerParams(vmem_limit_bytes=60 * 1024 * 1024),
        name="stacks",
    )(plan, *([gathered] * (steps + 1)))


def solution(mesh):
    placed = (P("fibre", "win", None), P(), P())
    return jax.shard_map(
        shards,
        mesh=mesh,
        in_specs=placed,
        out_specs=P(None, "win", None, None, "fibre"),
        check_vma=False,
    )
```

```python
import functools
import math

import jax
import jax.numpy as jnp
import ml_dtypes
import numpy as np
from jax import lax
from jax.experimental import pallas as pl
from jax.experimental.pallas import tpu as pltpu
from jax.sharding import PartitionSpec as P

FB = 256
FLO = 8
BLK = 64
ROWS = 16
MESH = pl.DeviceIdType.MESH


def tap_order(half_time):
    order = [0]
    for offset in range(1, half_time + 1):
        order += [offset, -offset]
    return order


@functools.lru_cache(maxsize=None)
def transform_table(samples, bins, half_time):
    index = np.arange(samples, dtype=np.int64)
    picks = np.zeros((-(-2 * half_time // ROWS) * ROWS, samples), ml_dtypes.bfloat16)
    for row in range(half_time):
        picks[row, row] = 1
        picks[half_time + row, samples - half_time + row] = 1
    blocks = []
    for start in range(0, FB, bins):
        wanted = FLO + start + np.arange(bins, dtype=np.int64)
        angles = (wanted[:, None] * index[None, :] % samples) * (2.0 * np.pi / samples)
        exact = np.concatenate([np.cos(angles), -np.sin(angles)])
        high = exact.astype(ml_dtypes.bfloat16)
        low = (exact - high.astype(np.float64)).astype(ml_dtypes.bfloat16)
        blocks += [high, low, picks]
    return np.concatenate(blocks)


@functools.lru_cache(maxsize=None)
def phase_table(samples, half_time):
    wanted = FLO + np.arange(FB, dtype=np.int64)
    angles = wanted[:, None] * np.arange(1, half_time + 1)[None, :] % samples * (2.0 * np.pi / samples)
    return np.concatenate([np.cos(angles), np.sin(angles)], axis=1).astype(np.float32)


def gather_orders(count):
    bits = [1 << place for place in range(1, count.bit_length() - 1)]
    return [bits + [1], bits[::-1] + [1]]


def spectra_kernel(
    fibres, wins, margin, half_time,
    taps_ref, phase_hbm, table_ref, strain_ref, out_ref,
    phase_ref, table_v, x_v, band_v, white_v,
    load_sem, halo_send, halo_recv, swap_send, swap_recv, keep_sem, gather_send, gather_recv,
):
    me = lax.axis_index("fibre")
    win = lax.axis_index("win")
    channels = strain_ref.shape[0]
    bins = white_v.shape[2]
    halo = (x_v.shape[0] - channels) // 2
    chan_taps = 2 * margin + 1
    order = tap_order(half_time)

    load_table = pltpu.make_async_copy(table_ref, table_v, load_sem.at[0])
    load_table.start()
    load_own = pltpu.make_async_copy(strain_ref, x_v.at[pl.ds(0, channels)], load_sem.at[1])
    load_own.start()
    load_phase = pltpu.make_async_copy(phase_hbm, phase_ref, load_sem.at[2])
    load_phase.start()

    barrier = pltpu.get_barrier_semaphore()
    for step in range(1, fibres):
        pl.semaphore_signal(barrier, inc=1, device_id={"fibre": lax.rem(me + step, fibres)}, device_id_type=MESH)
    for step in range(1, wins):
        pl.semaphore_signal(barrier, inc=1, device_id={"win": lax.rem(win + step, wins)}, device_id_type=MESH)

    own_pieces, halo_pieces = channels // ROWS, halo // ROWS
    slope = lax.broadcasted_iota(jnp.int32, (ROWS, channels), 0) - lax.broadcasted_iota(jnp.int32, (ROWS, channels), 1)

    def band_piece(piece, carry):
        start = jnp.where(
            piece < own_pieces, piece * ROWS,
            jnp.where(piece < own_pieces + halo_pieces, (piece - own_pieces) * ROWS - halo, (piece - halo_pieces) * ROWS),
        )
        lag = slope + (start + margin)
        totals = [jnp.zeros((ROWS, channels), jnp.float32)] * len(order)
        for tap in range(chan_taps):
            here = lag == tap
            totals = [
                jnp.where(here, taps_ref[tap, offset + half_time], total) for total, offset in zip(totals, order)
            ]
        rows = pl.ds(pl.multiple_of(piece * ROWS, ROWS), ROWS)
        for place, total in enumerate(totals):
            band_v[rows, place * channels : (place + 1) * channels] = total.astype(jnp.bfloat16)
        return carry

    lax.fori_loop(0, own_pieces + 2 * halo_pieces, band_piece, 0)

    pl.semaphore_wait(barrier, fibres + wins - 2)

    to_right = pltpu.make_async_remote_copy(
        src_ref=strain_ref.at[pl.ds(channels - halo, halo)], dst_ref=x_v.at[pl.ds(channels, halo)],
        send_sem=halo_send.at[0], recv_sem=halo_recv.at[0],
        device_id={"fibre": lax.rem(me + 1, fibres)}, device_id_type=MESH,
    )
    to_left = pltpu.make_async_remote_copy(
        src_ref=strain_ref.at[pl.ds(0, halo)], dst_ref=x_v.at[pl.ds(channels + halo, halo)],
        send_sem=halo_send.at[1], recv_sem=halo_recv.at[1],
        device_id={"fibre": lax.rem(me + fibres - 1, fibres)}, device_id_type=MESH,
    )
    first, last = me == 0, me == fibres - 1

    @pl.when(jnp.logical_not(last))
    def _():
        to_right.start()

    @pl.when(jnp.logical_not(first))
    def _():
        to_left.start()

    @pl.when(first)
    def _():
        x_v[channels : channels + halo, :] = jnp.zeros((halo, x_v.shape[1]), x_v.dtype)

    @pl.when(last)
    def _():
        x_v[channels + halo :, :] = jnp.zeros((halo, x_v.shape[1]), x_v.dtype)

    load_own.wait()

    @pl.when(jnp.logical_not(last))
    def _():
        to_right.wait_send()
        to_left.wait_recv()

    @pl.when(jnp.logical_not(first))
    def _():
        to_left.wait_send()
        to_right.wait_recv()

    load_table.wait()
    load_phase.wait()
    group_rows = table_v.shape[0] // wins

    def whiten_group(group):
        base = pl.multiple_of(group * group_rows, ROWS)
        spectra = lax.dot_general(
            table_v[pl.ds(base, group_rows), :], x_v[...], (((1,), (1,)), ((), ())),
            preferred_element_type=jnp.float32,
        )
        both = spectra[: 2 * bins] + spectra[2 * bins : 4 * bins]
        high = both.astype(jnp.bfloat16)
        low = (both - high.astype(jnp.float32)).astype(jnp.bfloat16)
        edges = spectra[4 * bins :].astype(jnp.bfloat16)
        parts = jnp.dot(
            jnp.concatenate([high, low, edges]), band_v[...], preferred_element_type=jnp.float32
        )
        tails = parts[4 * bins :]

        def tail(row, offset):
            place = order.index(offset)
            return tails[row : row + 1, place * channels : (place + 1) * channels]

        before = {m: sum(tail(u, m + u) for u in range(half_time - m + 1)) for m in range(1, half_time + 1)}
        after = {
            m: sum(tail(2 * half_time - v, -(v + m)) for v in range(1, half_time - m + 1)) for m in range(half_time)
        }
        shifted = parts[: 2 * bins] + parts[2 * bins : 4 * bins]
        real = shifted[:bins, :channels] - after[0]
        imag = shifted[bins:, :channels]
        bin_rows = pl.ds(pl.multiple_of(group * bins, bins), bins)
        for offset in range(1, half_time + 1):
            pair = shifted[:, (2 * offset - 1) * channels : (2 * offset + 1) * channels]
            ahead_re = pair[:bins, :channels] - before[offset]
            back_re = pair[:bins, channels:]
            if offset in after:
                back_re = back_re - after[offset]
            ahead_im, back_im = pair[bins:, :channels], pair[bins:, channels:]
            cos = phase_ref[bin_rows, offset - 1 : offset]
            sin = phase_ref[bin_rows, half_time + offset - 1 : half_time + offset]
            real += cos * (ahead_re + back_re) - sin * (ahead_im - back_im)
            imag += cos * (ahead_im + back_im) + sin * (ahead_re - back_re)
        magnitude = jnp.sqrt(real * real + imag * imag)
        for start in range(0, bins, BLK):
            level = jnp.mean(magnitude[start : start + BLK], axis=0, keepdims=True) + 1e-06
            factor = 1.0 / level
            white_v[group, 0, start : start + BLK] = (real[start : start + BLK] * factor).astype(jnp.bfloat16)
            white_v[group, 1, start : start + BLK] = (imag[start : start + BLK] * factor).astype(jnp.bfloat16)

    def swap(step):
        target = lax.rem(win + step, wins)
        return pltpu.make_async_remote_copy(
            src_ref=white_v.at[target], dst_ref=out_ref.at[me, win],
            send_sem=swap_send.at[step], recv_sem=swap_recv.at[step],
            device_id={"win": target}, device_id_type=MESH,
        )

    def swap_arrival(step):
        source = lax.rem(win + wins - step, wins)
        return pltpu.make_async_remote_copy(
            src_ref=white_v.at[win], dst_ref=out_ref.at[me, source],
            send_sem=swap_send.at[step], recv_sem=swap_recv.at[step],
            device_id={"win": source}, device_id_type=MESH,
        )

    def group_step(turn, carry):
        step = lax.rem(turn + 1, wins)
        whiten_group(lax.rem(win + step, wins))

        @pl.when(step != 0)
        def _():
            swap(step).start()

        return carry

    lax.fori_loop(0, wins, group_step, 0)
    keep = pltpu.make_async_copy(white_v.at[win], out_ref.at[me, win], keep_sem)
    keep.start()

    orders = gather_orders(fibres)
    arrival_order = [0] + sorted(range(1, wins), key=lambda step: min(step, wins - step))

    def hop(step, away, bit):
        block = lax.bitwise_xor(me, away)
        window = lax.rem(win + wins - step, wins)
        source = white_v.at[win] if step == 0 and away == 0 else out_ref.at[block, window]
        return pltpu.make_async_remote_copy(
            src_ref=source, dst_ref=out_ref.at[block, window],
            send_sem=gather_send.at[away ^ bit, step], recv_sem=gather_recv.at[away ^ bit, step],
            device_id={"fibre": lax.bitwise_xor(me, bit)}, device_id_type=MESH,
        )

    events = []
    for rank, step in enumerate(arrival_order):
        line = orders[rank % 2]
        for away in range(fibres):
            taken = [place for place, bit in enumerate(line) if away & bit]
            latest = max(taken, default=-1)
            events.append((rank + len(taken), rank, latest, away, step, line))
    events.sort(key=lambda event: event[:4])
    started = []
    for _, _, latest, away, step, line in events:
        if away:
            hop(step, away ^ line[latest], line[latest]).wait_recv()
        elif step:
            swap_arrival(step).wait_recv()
        for bit in line[latest + 1 :]:
            copy = hop(step, away, bit)
            copy.start()
            started.append(copy)
    keep.wait()
    for step in range(1, wins):
        swap(step).wait_send()
    for copy in started:
        copy.wait_send()


def stack_kernel(steps, scale, per_turn, plan_ref, gathered_ref, out_ref, blocks_v, left_v, right_v, result_v, load_sem, out_sem):
    wins, _, bins, channels = gathered_ref.shape[1:]
    depth = wins * 2 * ROWS
    exact = math.frexp(scale)[0] == 0.5
    loads = []
    for place in range(steps + 1):
        block = plan_ref[place] if place < steps else lax.axis_index("fibre")
        loads.append(pltpu.make_async_copy(gathered_ref.at[block], blocks_v.at[place], load_sem.at[place]))
        loads[-1].start()
    for load in loads:
        load.wait()
    row = lax.broadcasted_iota(jnp.int32, (ROWS, 2 * channels), 0)

    def write(turn, step):
        slot = lax.rem(turn, 2)
        return pltpu.make_async_copy(
            result_v.at[slot, step], out_ref.at[step, pl.ds(turn * per_turn, per_turn)], out_sem.at[slot, step]
        )

    def stack_turn(turn, carry):
        slot = lax.rem(turn, 2)
        first_bin = turn * per_turn

        @pl.when(lax.rem(first_bin, ROWS) == 0)
        def _():
            group = pl.ds(pl.multiple_of(first_bin, ROWS), ROWS)
            for step in range(steps):
                piece = blocks_v[step, :, :, group, :].reshape(depth, channels).astype(jnp.float32)
                if exact:
                    piece = piece * scale
                left_v[step * channels : (step + 1) * channels, :] = piece.T.astype(jnp.bfloat16)
            real = blocks_v[steps, :, 0, group, :]
            imag = blocks_v[steps, :, 1, group, :]
            right_v[:, :channels] = jnp.stack([real, imag], axis=1).reshape(depth, channels)
            right_v[:, channels:] = jnp.stack([imag, -real], axis=1).reshape(depth, channels)

        @pl.when(turn >= 2)
        def _():
            for step in range(steps):
                write(turn - 2, step).wait()

        right = right_v[...].reshape(wins * 2, ROWS, 2 * channels)
        left = left_v[...]
        for place in range(per_turn):
            here = jnp.where(row == lax.rem(first_bin + place, ROWS), 1.0, 0.0).astype(jnp.bfloat16)
            one_bin = (right * here[None]).reshape(depth, 2 * channels)
            result = jnp.dot(left, one_bin, preferred_element_type=jnp.float32)
            if not exact:
                result = result * scale
            result = result.astype(jnp.bfloat16)
            for step in range(steps):
                result_v[slot, step, place, 0] = result[step * channels : (step + 1) * channels, :channels]
                result_v[slot, step, place, 1] = result[step * channels : (step + 1) * channels, channels:]
        for step in range(steps):
            write(turn, step).start()
        return carry

    turns = bins // per_turn
    lax.fori_loop(0, turns, stack_turn, 0)
    for turn in (turns - 2, turns - 1):
        for step in range(steps):
            write(turn, step).wait()


def shards(strain, kernel, plan):
    fibres, wins = lax.axis_size("fibre"), lax.axis_size("win")
    channels, own_windows, samples = strain.shape
    margin, half_time = kernel.shape[0] // 2, kernel.shape[1] // 2
    bins = FB // wins
    halo = -(-margin // ROWS) * ROWS
    assert own_windows == 1 and bins % BLK == 0 and fibres & (fibres - 1) == 0
    table = transform_table(samples, bins, half_time)
    phases = phase_table(samples, half_time)
    any_space = pl.BlockSpec(memory_space=pl.ANY)
    gathered = pl.pallas_call(
        functools.partial(spectra_kernel, fibres, wins, margin, half_time),
        out_shape=jax.ShapeDtypeStruct((fibres, wins, 2, bins, channels), jnp.bfloat16),
        in_specs=[
            pl.BlockSpec(memory_space=pltpu.SMEM),
            pl.BlockSpec(memory_space=pltpu.HBM),
            pl.BlockSpec(memory_space=pltpu.HBM),
            pl.BlockSpec(memory_space=pltpu.HBM),
        ],
        out_specs=any_space,
        scratch_shapes=[
            pltpu.VMEM(phases.shape, jnp.float32),
            pltpu.VMEM(table.shape, jnp.bfloat16),
            pltpu.VMEM((channels + 2 * halo, samples), jnp.bfloat16),
            pltpu.VMEM((channels + 2 * halo, kernel.shape[1] * channels), jnp.bfloat16),
            pltpu.VMEM((wins, 2, bins, channels), jnp.bfloat16),
            pltpu.SemaphoreType.DMA((3,)),
            pltpu.SemaphoreType.DMA((2,)),
            pltpu.SemaphoreType.DMA((2,)),
            pltpu.SemaphoreType.DMA((wins,)),
            pltpu.SemaphoreType.DMA((wins,)),
            pltpu.SemaphoreType.DMA,
            pltpu.SemaphoreType.DMA((fibres, wins)),
            pltpu.SemaphoreType.DMA((fibres, wins)),
        ],
        compiler_params=pltpu.CompilerParams(
            collective_id=0, has_side_effects=True, vmem_limit_bytes=60 * 1024 * 1024
        ),
        name="spectra",
    )(kernel.astype(jnp.float32), jnp.asarray(phases), jnp.asarray(table), strain.reshape(channels, samples))

    steps = plan.shape[0]
    per_turn = 4
    return pl.pallas_call(
        functools.partial(stack_kernel, steps, 1.0 / math.sqrt(wins * own_windows), per_turn),
        out_shape=jax.ShapeDtypeStruct((steps, bins, 2, channels, channels), jnp.bfloat16),
        in_specs=[pl.BlockSpec(memory_space=pltpu.SMEM), any_space],
        out_specs=any_space,
        scratch_shapes=[
            pltpu.VMEM((steps + 1, wins, 2, bins, channels), jnp.bfloat16),
            pltpu.VMEM((steps * channels, wins * 2 * ROWS), jnp.bfloat16),
            pltpu.VMEM((wins * 2 * ROWS, 2 * channels), jnp.bfloat16),
            pltpu.VMEM((2, steps, per_turn, 2, channels, channels), jnp.bfloat16),
            pltpu.SemaphoreType.DMA((steps + 1,)),
            pltpu.SemaphoreType.DMA((2, steps)),
        ],
        compiler_params=pltpu.CompilerParams(vmem_limit_bytes=60 * 1024 * 1024),
        name="stacks",
    )(plan, gathered)


def solution(mesh):
    placed = (P("fibre", "win", None), P(), P())
    return jax.shard_map(
        shards,
        mesh=mesh,
        in_specs=placed,
        out_specs=P(None, "win", None, None, "fibre"),
        check_vma=False,
    )
```

```python
import functools
import math

import jax
import jax.numpy as jnp
import ml_dtypes
import numpy as np
from jax import lax
from jax.experimental import pallas as pl
from jax.experimental.pallas import tpu as pltpu
from jax.sharding import PartitionSpec as P

FB = 256
FLO = 8
BLK = 64
ROWS = 16
MESH = pl.DeviceIdType.MESH


def tap_order(half_time):
    order = [0]
    for offset in range(1, half_time + 1):
        order += [offset, -offset]
    return order


@functools.lru_cache(maxsize=None)
def transform_table(samples, bins, half_time):
    index = np.arange(samples, dtype=np.int64)
    picks = np.zeros((-(-2 * half_time // ROWS) * ROWS, samples), ml_dtypes.bfloat16)
    for row in range(half_time):
        picks[row, row] = 1
        picks[half_time + row, samples - half_time + row] = 1
    blocks = []
    for start in range(0, FB, bins):
        wanted = FLO + start + np.arange(bins, dtype=np.int64)
        angles = (wanted[:, None] * index[None, :] % samples) * (2.0 * np.pi / samples)
        exact = np.concatenate([np.cos(angles), -np.sin(angles)])
        high = exact.astype(ml_dtypes.bfloat16)
        low = (exact - high.astype(np.float64)).astype(ml_dtypes.bfloat16)
        blocks += [high, low, picks]
    return np.concatenate(blocks)


@functools.lru_cache(maxsize=None)
def phase_table(samples, half_time):
    wanted = FLO + np.arange(FB, dtype=np.int64)
    angles = wanted[:, None] * np.arange(1, half_time + 1)[None, :] % samples * (2.0 * np.pi / samples)
    return np.concatenate([np.cos(angles), np.sin(angles)], axis=1).astype(np.float32)


def gather_orders(count):
    bits = [1 << place for place in range(1, count.bit_length() - 1)]
    return [bits + [1], bits[::-1] + [1]]


def spectra_kernel(
    fibres, wins, margin, half_time,
    taps_ref, phase_hbm, table_ref, strain_ref, out_ref,
    phase_ref, table_v, x_v, xt_v, band_v, white_v,
    load_sem, halo_send, halo_recv, swap_send, swap_recv, keep_sem, gather_send, gather_recv,
):
    me = lax.axis_index("fibre")
    win = lax.axis_index("win")
    channels = strain_ref.shape[0]
    bins = white_v.shape[2]
    halo = (x_v.shape[0] - channels) // 2
    chan_taps = 2 * margin + 1
    order = tap_order(half_time)

    load_table = pltpu.make_async_copy(table_ref, table_v, load_sem.at[0])
    load_table.start()
    load_own = pltpu.make_async_copy(strain_ref, x_v.at[pl.ds(0, channels)], load_sem.at[1])
    load_own.start()
    load_phase = pltpu.make_async_copy(phase_hbm, phase_ref, load_sem.at[2])
    load_phase.start()

    barrier = pltpu.get_barrier_semaphore()
    for step in range(1, fibres):
        pl.semaphore_signal(barrier, inc=1, device_id={"fibre": lax.rem(me + step, fibres)}, device_id_type=MESH)
    for step in range(1, wins):
        pl.semaphore_signal(barrier, inc=1, device_id={"win": lax.rem(win + step, wins)}, device_id_type=MESH)
    pl.semaphore_wait(barrier, fibres + wins - 2)

    to_right = pltpu.make_async_remote_copy(
        src_ref=strain_ref.at[pl.ds(channels - halo, halo)], dst_ref=x_v.at[pl.ds(channels, halo)],
        send_sem=halo_send.at[0], recv_sem=halo_recv.at[0],
        device_id={"fibre": lax.rem(me + 1, fibres)}, device_id_type=MESH,
    )
    to_left = pltpu.make_async_remote_copy(
        src_ref=strain_ref.at[pl.ds(0, halo)], dst_ref=x_v.at[pl.ds(channels + halo, halo)],
        send_sem=halo_send.at[1], recv_sem=halo_recv.at[1],
        device_id={"fibre": lax.rem(me + fibres - 1, fibres)}, device_id_type=MESH,
    )
    first, last = me == 0, me == fibres - 1

    @pl.when(jnp.logical_not(last))
    def _():
        to_right.start()

    @pl.when(jnp.logical_not(first))
    def _():
        to_left.start()

    @pl.when(first)
    def _():
        x_v[channels : channels + halo, :] = jnp.zeros((halo, x_v.shape[1]), x_v.dtype)

    @pl.when(last)
    def _():
        x_v[channels + halo :, :] = jnp.zeros((halo, x_v.shape[1]), x_v.dtype)

    load_own.wait()

    def turn_over(piece, carry):
        columns = pl.ds(pl.multiple_of(piece * 256, 256), 256)
        xt_v[columns, :channels] = x_v[:channels, columns].astype(jnp.float32).T.astype(jnp.bfloat16)
        return carry

    lax.fori_loop(0, x_v.shape[1] // 256, turn_over, 0)

    def band_rows(first_row, rows, source):
        lag = source - lax.broadcasted_iota(jnp.int32, (rows, channels), 1) + margin
        totals = [jnp.zeros((rows, channels), jnp.float32)] * len(order)
        for tap in range(chan_taps):
            here = lag == tap
            totals = [
                jnp.where(here, taps_ref[tap, offset + half_time], total) for total, offset in zip(totals, order)
            ]
        for place, total in enumerate(totals):
            band_v[pl.ds(first_row, rows), place * channels : (place + 1) * channels] = total.astype(jnp.bfloat16)

    def own_rows(piece, carry):
        first_row = pl.multiple_of(piece * 2 * ROWS, 2 * ROWS)
        band_rows(first_row, 2 * ROWS, lax.broadcasted_iota(jnp.int32, (2 * ROWS, channels), 0) + first_row)
        return carry

    lax.fori_loop(0, channels // (2 * ROWS), own_rows, 0)
    row = lax.broadcasted_iota(jnp.int32, (2 * halo, channels), 0)
    band_rows(channels, 2 * halo, row - halo + jnp.where(row < halo, 0, channels))

    @pl.when(jnp.logical_not(last))
    def _():
        to_right.wait_send()
        to_left.wait_recv()

    @pl.when(jnp.logical_not(first))
    def _():
        to_left.wait_send()
        to_right.wait_recv()

    xt_v[:, channels:] = x_v[channels:, :].astype(jnp.float32).T.astype(jnp.bfloat16)
    load_table.wait()
    load_phase.wait()
    group_rows = table_v.shape[0] // wins

    def whiten_group(group):
        base = pl.multiple_of(group * group_rows, ROWS)
        spectra = jnp.dot(
            table_v[pl.ds(base, group_rows), :], xt_v[...], preferred_element_type=jnp.float32
        )
        both = spectra[: 2 * bins] + spectra[2 * bins : 4 * bins]
        high = both.astype(jnp.bfloat16)
        low = (both - high.astype(jnp.float32)).astype(jnp.bfloat16)
        edges = spectra[4 * bins :].astype(jnp.bfloat16)
        parts = jnp.dot(
            jnp.concatenate([high, low, edges]), band_v[...], preferred_element_type=jnp.float32
        )
        tails = parts[4 * bins :]

        def tail(row, offset):
            place = order.index(offset)
            return tails[row : row + 1, place * channels : (place + 1) * channels]

        before = {m: sum(tail(u, m + u) for u in range(half_time - m + 1)) for m in range(1, half_time + 1)}
        after = {
            m: sum(tail(2 * half_time - v, -(v + m)) for v in range(1, half_time - m + 1)) for m in range(half_time)
        }
        shifted = parts[: 2 * bins] + parts[2 * bins : 4 * bins]
        real = shifted[:bins, :channels] - after[0]
        imag = shifted[bins:, :channels]
        bin_rows = pl.ds(pl.multiple_of(group * bins, bins), bins)
        for offset in range(1, half_time + 1):
            pair = shifted[:, (2 * offset - 1) * channels : (2 * offset + 1) * channels]
            ahead_re = pair[:bins, :channels] - before[offset]
            back_re = pair[:bins, channels:]
            if offset in after:
                back_re = back_re - after[offset]
            ahead_im, back_im = pair[bins:, :channels], pair[bins:, channels:]
            cos = phase_ref[bin_rows, offset - 1 : offset]
            sin = phase_ref[bin_rows, half_time + offset - 1 : half_time + offset]
            real += cos * (ahead_re + back_re) - sin * (ahead_im - back_im)
            imag += cos * (ahead_im + back_im) + sin * (ahead_re - back_re)
        magnitude = jnp.sqrt(real * real + imag * imag)
        for start in range(0, bins, BLK):
            level = jnp.mean(magnitude[start : start + BLK], axis=0, keepdims=True) + 1e-06
            factor = 1.0 / level
            white_v[group, 0, start : start + BLK] = (real[start : start + BLK] * factor).astype(jnp.bfloat16)
            white_v[group, 1, start : start + BLK] = (imag[start : start + BLK] * factor).astype(jnp.bfloat16)

    def swap(step):
        target = lax.rem(win + step, wins)
        return pltpu.make_async_remote_copy(
            src_ref=white_v.at[target], dst_ref=out_ref.at[me, win],
            send_sem=swap_send.at[step], recv_sem=swap_recv.at[step],
            device_id={"win": target}, device_id_type=MESH,
        )

    def swap_arrival(step):
        source = lax.rem(win + wins - step, wins)
        return pltpu.make_async_remote_copy(
            src_ref=white_v.at[win], dst_ref=out_ref.at[me, source],
            send_sem=swap_send.at[step], recv_sem=swap_recv.at[step],
            device_id={"win": source}, device_id_type=MESH,
        )

    def group_step(turn, carry):
        step = lax.rem(turn + 1, wins)
        whiten_group(lax.rem(win + step, wins))

        @pl.when(step != 0)
        def _():
            swap(step).start()

        return carry

    lax.fori_loop(0, wins, group_step, 0)
    keep = pltpu.make_async_copy(white_v.at[win], out_ref.at[me, win], keep_sem)
    keep.start()

    orders = gather_orders(fibres)
    arrival_order = [0] + sorted(range(1, wins), key=lambda step: min(step, wins - step))

    def hop(step, away, bit):
        block = lax.bitwise_xor(me, away)
        window = lax.rem(win + wins - step, wins)
        source = white_v.at[win] if step == 0 and away == 0 else out_ref.at[block, window]
        return pltpu.make_async_remote_copy(
            src_ref=source, dst_ref=out_ref.at[block, window],
            send_sem=gather_send.at[away ^ bit, step], recv_sem=gather_recv.at[away ^ bit, step],
            device_id={"fibre": lax.bitwise_xor(me, bit)}, device_id_type=MESH,
        )

    events = []
    for rank, step in enumerate(arrival_order):
        line = orders[rank % 2]
        for away in range(fibres):
            taken = [place for place, bit in enumerate(line) if away & bit]
            latest = max(taken, default=-1)
            events.append((rank + len(taken), rank, latest, away, step, line))
    events.sort(key=lambda event: event[:4])
    started = []
    for _, _, latest, away, step, line in events:
        if away:
            hop(step, away ^ line[latest], line[latest]).wait_recv()
        elif step:
            swap_arrival(step).wait_recv()
        for bit in line[latest + 1 :]:
            copy = hop(step, away, bit)
            copy.start()
            started.append(copy)
    keep.wait()
    for step in range(1, wins):
        swap(step).wait_send()
    for copy in started:
        copy.wait_send()


def stack_kernel(steps, scale, per_turn, plan_ref, gathered_ref, out_ref, blocks_v, left_v, right_v, result_v, load_sem, out_sem):
    wins, _, bins, channels = gathered_ref.shape[1:]
    depth = wins * 2 * ROWS
    exact = math.frexp(scale)[0] == 0.5
    loads = []
    for place in range(steps + 1):
        block = plan_ref[place] if place < steps else lax.axis_index("fibre")
        loads.append(pltpu.make_async_copy(gathered_ref.at[block], blocks_v.at[place], load_sem.at[place]))
        loads[-1].start()
    for load in loads:
        load.wait()
    row = lax.broadcasted_iota(jnp.int32, (ROWS, 2 * channels), 0)

    def write(turn, step):
        slot = lax.rem(turn, 2)
        return pltpu.make_async_copy(
            result_v.at[slot, step], out_ref.at[step, pl.ds(turn * per_turn, per_turn)], out_sem.at[slot, step]
        )

    def stack_turn(turn, carry):
        slot = lax.rem(turn, 2)
        first_bin = turn * per_turn

        @pl.when(lax.rem(first_bin, ROWS) == 0)
        def _():
            group = pl.ds(pl.multiple_of(first_bin, ROWS), ROWS)
            for step in range(steps):
                piece = blocks_v[step, :, :, group, :].reshape(depth, channels).astype(jnp.float32)
                if exact:
                    piece = piece * scale
                left_v[step * channels : (step + 1) * channels, :] = piece.T.astype(jnp.bfloat16)
            real = blocks_v[steps, :, 0, group, :]
            imag = blocks_v[steps, :, 1, group, :]
            right_v[:, :channels] = jnp.stack([real, imag], axis=1).reshape(depth, channels)
            right_v[:, channels:] = jnp.stack([imag, -real], axis=1).reshape(depth, channels)

        @pl.when(turn >= 2)
        def _():
            for step in range(steps):
                write(turn - 2, step).wait()

        right = right_v[...].reshape(wins * 2, ROWS, 2 * channels)
        left = left_v[...]
        for pair in range(0, per_turn, 2):
            columns = []
            for place in (pair, pair + 1):
                here = jnp.where(row == lax.rem(first_bin + place, ROWS), 1.0, 0.0).astype(jnp.bfloat16)
                columns.append((right * here[None]).reshape(depth, 2 * channels))
            result = jnp.dot(left, jnp.concatenate(columns, axis=1), preferred_element_type=jnp.float32)
            if not exact:
                result = result * scale
            result = result.astype(jnp.bfloat16)
            for step in range(steps):
                rows = result[step * channels : (step + 1) * channels]
                for part in range(4):
                    result_v[slot, step, pair + part // 2, part % 2] = rows[:, part * channels : (part + 1) * channels]
        for step in range(steps):
            write(turn, step).start()
        return carry

    turns = bins // per_turn
    lax.fori_loop(0, turns, stack_turn, 0)
    for turn in (turns - 2, turns - 1):
        for step in range(steps):
            write(turn, step).wait()


def shards(strain, kernel, plan):
    fibres, wins = lax.axis_size("fibre"), lax.axis_size("win")
    channels, own_windows, samples = strain.shape
    margin, half_time = kernel.shape[0] // 2, kernel.shape[1] // 2
    bins = FB // wins
    halo = -(-margin // ROWS) * ROWS
    assert own_windows == 1 and bins % BLK == 0 and fibres & (fibres - 1) == 0
    table = transform_table(samples, bins, half_time)
    phases = phase_table(samples, half_time)
    any_space = pl.BlockSpec(memory_space=pl.ANY)
    gathered = pl.pallas_call(
        functools.partial(spectra_kernel, fibres, wins, margin, half_time),
        out_shape=jax.ShapeDtypeStruct((fibres, wins, 2, bins, channels), jnp.bfloat16),
        in_specs=[
            pl.BlockSpec(memory_space=pltpu.SMEM),
            pl.BlockSpec(memory_space=pltpu.HBM),
            pl.BlockSpec(memory_space=pltpu.HBM),
            pl.BlockSpec(memory_space=pltpu.HBM),
        ],
        out_specs=any_space,
        scratch_shapes=[
            pltpu.VMEM(phases.shape, jnp.float32),
            pltpu.VMEM(table.shape, jnp.bfloat16),
            pltpu.VMEM((channels + 2 * halo, samples), jnp.bfloat16),
            pltpu.VMEM((samples, channels + 2 * halo), jnp.bfloat16),
            pltpu.VMEM((channels + 2 * halo, kernel.shape[1] * channels), jnp.bfloat16),
            pltpu.VMEM((wins, 2, bins, channels), jnp.bfloat16),
            pltpu.SemaphoreType.DMA((3,)),
            pltpu.SemaphoreType.DMA((2,)),
            pltpu.SemaphoreType.DMA((2,)),
            pltpu.SemaphoreType.DMA((wins,)),
            pltpu.SemaphoreType.DMA((wins,)),
            pltpu.SemaphoreType.DMA,
            pltpu.SemaphoreType.DMA((fibres, wins)),
            pltpu.SemaphoreType.DMA((fibres, wins)),
        ],
        compiler_params=pltpu.CompilerParams(
            collective_id=0, has_side_effects=True, vmem_limit_bytes=60 * 1024 * 1024
        ),
        name="spectra",
    )(kernel.astype(jnp.float32), jnp.asarray(phases), jnp.asarray(table), strain.reshape(channels, samples))

    steps = plan.shape[0]
    per_turn = 8
    return pl.pallas_call(
        functools.partial(stack_kernel, steps, 1.0 / math.sqrt(wins * own_windows), per_turn),
        out_shape=jax.ShapeDtypeStruct((steps, bins, 2, channels, channels), jnp.bfloat16),
        in_specs=[pl.BlockSpec(memory_space=pltpu.SMEM), any_space],
        out_specs=any_space,
        scratch_shapes=[
            pltpu.VMEM((steps + 1, wins, 2, bins, channels), jnp.bfloat16),
            pltpu.VMEM((steps * channels, wins * 2 * ROWS), jnp.bfloat16),
            pltpu.VMEM((wins * 2 * ROWS, 2 * channels), jnp.bfloat16),
            pltpu.VMEM((2, steps, per_turn, 2, channels, channels), jnp.bfloat16),
            pltpu.SemaphoreType.DMA((steps + 1,)),
            pltpu.SemaphoreType.DMA((2, steps)),
        ],
        compiler_params=pltpu.CompilerParams(vmem_limit_bytes=60 * 1024 * 1024),
        name="stacks",
    )(plan, gathered)


def solution(mesh):
    placed = (P("fibre", "win", None), P(), P())
    return jax.shard_map(
        shards,
        mesh=mesh,
        in_specs=placed,
        out_specs=P(None, "win", None, None, "fibre"),
        check_vma=False,
    )
```

```python
import functools
import math

import jax
import jax.numpy as jnp
import ml_dtypes
import numpy as np
from jax import lax
from jax.experimental import pallas as pl
from jax.experimental.pallas import tpu as pltpu
from jax.sharding import PartitionSpec as P

FB = 256
FLO = 8
BLK = 64
ROWS = 16
MESH = pl.DeviceIdType.MESH


def tap_order(half_time):
    order = [0]
    for offset in range(1, half_time + 1):
        order += [offset, -offset]
    return order


@functools.lru_cache(maxsize=None)
def transform_table(samples, bins, half_time):
    index = np.arange(samples, dtype=np.int64)
    picks = np.zeros((-(-2 * half_time // ROWS) * ROWS, samples), ml_dtypes.bfloat16)
    for row in range(half_time):
        picks[row, row] = 1
        picks[half_time + row, samples - half_time + row] = 1
    blocks = []
    for start in range(0, FB, bins):
        wanted = FLO + start + np.arange(bins, dtype=np.int64)
        angles = (wanted[:, None] * index[None, :] % samples) * (2.0 * np.pi / samples)
        exact = np.concatenate([np.cos(angles), -np.sin(angles)])
        high = exact.astype(ml_dtypes.bfloat16)
        low = (exact - high.astype(np.float64)).astype(ml_dtypes.bfloat16)
        blocks += [high, low, picks]
    return np.concatenate(blocks)


@functools.lru_cache(maxsize=None)
def phase_table(samples, half_time):
    wanted = FLO + np.arange(FB, dtype=np.int64)
    angles = wanted[:, None] * np.arange(1, half_time + 1)[None, :] % samples * (2.0 * np.pi / samples)
    return np.concatenate([np.cos(angles), np.sin(angles)], axis=1).astype(np.float32)


def gather_orders(count):
    bits = [1 << place for place in range(1, count.bit_length() - 1)]
    return [bits + [1], bits[::-1] + [1]]


def spectra_kernel(
    fibres, wins, margin, half_time,
    taps_ref, phase_hbm, table_ref, strain_ref, out_ref,
    phase_ref, table_v, x_v, xt_v, band_v, white_v, held_v,
    load_sem, halo_send, halo_recv, swap_send, swap_recv, keep_sem, gather_send, gather_recv,
):
    me = lax.axis_index("fibre")
    win = lax.axis_index("win")
    channels = strain_ref.shape[0]
    bins = white_v.shape[2]
    halo = (x_v.shape[0] - channels) // 2
    chan_taps = 2 * margin + 1
    order = tap_order(half_time)

    load_table = pltpu.make_async_copy(table_ref, table_v, load_sem.at[0])
    load_table.start()
    load_own = pltpu.make_async_copy(strain_ref, x_v.at[pl.ds(0, channels)], load_sem.at[1])
    load_own.start()
    load_phase = pltpu.make_async_copy(phase_hbm, phase_ref, load_sem.at[2])
    load_phase.start()

    barrier = pltpu.get_barrier_semaphore()
    for step in range(1, fibres):
        pl.semaphore_signal(barrier, inc=1, device_id={"fibre": lax.rem(me + step, fibres)}, device_id_type=MESH)
    for step in range(1, wins):
        pl.semaphore_signal(barrier, inc=1, device_id={"win": lax.rem(win + step, wins)}, device_id_type=MESH)
    pl.semaphore_wait(barrier, fibres + wins - 2)

    to_right = pltpu.make_async_remote_copy(
        src_ref=strain_ref.at[pl.ds(channels - halo, halo)], dst_ref=x_v.at[pl.ds(channels, halo)],
        send_sem=halo_send.at[0], recv_sem=halo_recv.at[0],
        device_id={"fibre": lax.rem(me + 1, fibres)}, device_id_type=MESH,
    )
    to_left = pltpu.make_async_remote_copy(
        src_ref=strain_ref.at[pl.ds(0, halo)], dst_ref=x_v.at[pl.ds(channels + halo, halo)],
        send_sem=halo_send.at[1], recv_sem=halo_recv.at[1],
        device_id={"fibre": lax.rem(me + fibres - 1, fibres)}, device_id_type=MESH,
    )
    first, last = me == 0, me == fibres - 1

    @pl.when(jnp.logical_not(last))
    def _():
        to_right.start()

    @pl.when(jnp.logical_not(first))
    def _():
        to_left.start()

    @pl.when(first)
    def _():
        x_v[channels : channels + halo, :] = jnp.zeros((halo, x_v.shape[1]), x_v.dtype)

    @pl.when(last)
    def _():
        x_v[channels + halo :, :] = jnp.zeros((halo, x_v.shape[1]), x_v.dtype)

    load_own.wait()

    def turn_over(piece, carry):
        columns = pl.ds(pl.multiple_of(piece * 256, 256), 256)
        xt_v[columns, :channels] = x_v[:channels, columns].astype(jnp.float32).T.astype(jnp.bfloat16)
        return carry

    lax.fori_loop(0, x_v.shape[1] // 256, turn_over, 0)

    def band_rows(first_row, rows, source):
        lag = source - lax.broadcasted_iota(jnp.int32, (rows, channels), 1) + margin
        totals = [jnp.zeros((rows, channels), jnp.float32)] * len(order)
        for tap in range(chan_taps):
            here = lag == tap
            totals = [
                jnp.where(here, taps_ref[tap, offset + half_time], total) for total, offset in zip(totals, order)
            ]
        for place, total in enumerate(totals):
            band_v[pl.ds(first_row, rows), place * channels : (place + 1) * channels] = total.astype(jnp.bfloat16)

    def own_rows(piece, carry):
        first_row = pl.multiple_of(piece * 2 * ROWS, 2 * ROWS)
        band_rows(first_row, 2 * ROWS, lax.broadcasted_iota(jnp.int32, (2 * ROWS, channels), 0) + first_row)
        return carry

    lax.fori_loop(0, channels // (2 * ROWS), own_rows, 0)
    row = lax.broadcasted_iota(jnp.int32, (2 * halo, channels), 0)
    band_rows(channels, 2 * halo, row - halo + jnp.where(row < halo, 0, channels))

    @pl.when(jnp.logical_not(last))
    def _():
        to_right.wait_send()
        to_left.wait_recv()

    @pl.when(jnp.logical_not(first))
    def _():
        to_left.wait_send()
        to_right.wait_recv()

    xt_v[:, channels:] = x_v[channels:, :].astype(jnp.float32).T.astype(jnp.bfloat16)
    load_table.wait()
    load_phase.wait()
    group_rows = table_v.shape[0] // wins

    def whiten_group(group, into):
        base = pl.multiple_of(group * group_rows, ROWS)
        spectra = jnp.dot(
            table_v[pl.ds(base, group_rows), :], xt_v[...], preferred_element_type=jnp.float32
        )
        both = spectra[: 2 * bins] + spectra[2 * bins : 4 * bins]
        high = both.astype(jnp.bfloat16)
        low = (both - high.astype(jnp.float32)).astype(jnp.bfloat16)
        edges = spectra[4 * bins :].astype(jnp.bfloat16)
        parts = jnp.dot(
            jnp.concatenate([high, low, edges]), band_v[...], preferred_element_type=jnp.float32
        )
        tails = parts[4 * bins :]

        def tail(row, offset):
            place = order.index(offset)
            return tails[row : row + 1, place * channels : (place + 1) * channels]

        before = {m: sum(tail(u, m + u) for u in range(half_time - m + 1)) for m in range(1, half_time + 1)}
        after = {
            m: sum(tail(2 * half_time - v, -(v + m)) for v in range(1, half_time - m + 1)) for m in range(half_time)
        }
        shifted = parts[: 2 * bins] + parts[2 * bins : 4 * bins]
        real = shifted[:bins, :channels] - after[0]
        imag = shifted[bins:, :channels]
        bin_rows = pl.ds(pl.multiple_of(group * bins, bins), bins)
        for offset in range(1, half_time + 1):
            pair = shifted[:, (2 * offset - 1) * channels : (2 * offset + 1) * channels]
            ahead_re = pair[:bins, :channels] - before[offset]
            back_re = pair[:bins, channels:]
            if offset in after:
                back_re = back_re - after[offset]
            ahead_im, back_im = pair[bins:, :channels], pair[bins:, channels:]
            cos = phase_ref[bin_rows, offset - 1 : offset]
            sin = phase_ref[bin_rows, half_time + offset - 1 : half_time + offset]
            real += cos * (ahead_re + back_re) - sin * (ahead_im - back_im)
            imag += cos * (ahead_im + back_im) + sin * (ahead_re - back_re)
        magnitude = jnp.sqrt(real * real + imag * imag)
        for start in range(0, bins, BLK):
            level = jnp.mean(magnitude[start : start + BLK], axis=0, keepdims=True) + 1e-06
            factor = 1.0 / level
            into[0, start : start + BLK] = (real[start : start + BLK] * factor).astype(jnp.bfloat16)
            into[1, start : start + BLK] = (imag[start : start + BLK] * factor).astype(jnp.bfloat16)

    def swap(step):
        target = lax.rem(win + step, wins)
        return pltpu.make_async_remote_copy(
            src_ref=white_v.at[target], dst_ref=held_v.at[me, win],
            send_sem=swap_send.at[step], recv_sem=swap_recv.at[step],
            device_id={"win": target}, device_id_type=MESH,
        )

    def swap_arrival(step):
        source = lax.rem(win + wins - step, wins)
        return pltpu.make_async_remote_copy(
            src_ref=white_v.at[win], dst_ref=held_v.at[me, source],
            send_sem=swap_send.at[step], recv_sem=swap_recv.at[step],
            device_id={"win": source}, device_id_type=MESH,
        )

    orders = gather_orders(fibres)

    def hop(step, away, bit):
        block = lax.bitwise_xor(me, away)
        window = lax.rem(win + wins - step, wins)
        return pltpu.make_async_remote_copy(
            src_ref=held_v.at[block, window], dst_ref=held_v.at[block, window],
            send_sem=gather_send.at[away ^ bit, step], recv_sem=gather_recv.at[away ^ bit, step],
            device_id={"fibre": lax.bitwise_xor(me, bit)}, device_id_type=MESH,
        )

    started = []

    def settle(step, away):
        line = orders[step % 2]
        latest = max([place for place, bit in enumerate(line) if away & bit], default=-1)
        if away:
            hop(step, away ^ line[latest], line[latest]).wait_recv()
        elif step:
            swap_arrival(step).wait_recv()
        for bit in line[latest + 1 :]:
            copy = hop(step, away, bit)
            copy.start()
            started.append(copy)
        block, window = lax.bitwise_xor(me, away), lax.rem(win + wins - step, wins)
        pltpu.make_async_copy(held_v.at[block, window], out_ref.at[block, window], keep_sem).start()

    events = sorted(
        (step + away.bit_count(), step, [away & bit != 0 for bit in orders[step % 2]][::-1], away)
        for step in range(wins) for away in range(fibres)
    )
    for turn in range(wins):
        if turn:
            target = lax.rem(win + turn, wins)
            whiten_group(target, white_v.at[target])
            swap(turn).start()
        else:
            whiten_group(win, held_v.at[me, win])
        due = [event for event in events if event[0] + (2 if event[1] else 1 if event[3] else 0) <= turn]
        events = [event for event in events if event not in due]
        for _, step, _, away in due:
            settle(step, away)
    for _, step, _, away in events:
        settle(step, away)
    for step in range(1, wins):
        swap(step).wait_send()
    for copy in started:
        copy.wait_send()
    pltpu.make_async_copy(held_v, out_ref, keep_sem).wait()


def stack_kernel(steps, scale, plan_ref, gathered_ref, out_ref, blocks_v, left_v, right_v, result_v, load_sem, out_sem):
    wins, _, bins, channels = gathered_ref.shape[1:]
    depth = wins * 2 * ROWS
    exact = math.frexp(scale)[0] == 0.5
    loads = []
    for place in range(steps + 1):
        block = plan_ref[place] if place < steps else lax.axis_index("fibre")
        loads.append(pltpu.make_async_copy(gathered_ref.at[block], blocks_v.at[place], load_sem.at[place]))
        loads[-1].start()
    for load in loads:
        load.wait()
    row = lax.broadcasted_iota(jnp.int32, (ROWS, 2 * channels), 0)

    pairs = ROWS // 2

    def write(group, pair):
        bin_pair = pl.ds(group * ROWS + 2 * pair, 2)
        return pltpu.make_async_copy(result_v.at[pair], out_ref.at[:, bin_pair], out_sem.at[pair])

    def stack_group(group, carry):
        rows = pl.ds(pl.multiple_of(group * ROWS, ROWS), ROWS)
        for step in range(steps):
            piece = blocks_v[step, :, :, rows, :].reshape(depth, channels).astype(jnp.float32)
            if exact:
                piece = piece * scale
            left_v[step * channels : (step + 1) * channels, :] = piece.T.astype(jnp.bfloat16)
        real = blocks_v[steps, :, 0, rows, :]
        imag = blocks_v[steps, :, 1, rows, :]
        right_v[:, :channels] = jnp.stack([real, imag], axis=1).reshape(depth, channels)
        right_v[:, channels:] = jnp.stack([imag, -real], axis=1).reshape(depth, channels)
        right = right_v[...].reshape(wins * 2, ROWS, 2 * channels)
        left = left_v[...]
        for pair in range(pairs):
            columns = []
            for place in (2 * pair, 2 * pair + 1):
                here = jnp.where(row == place, 1.0, 0.0).astype(jnp.bfloat16)
                columns.append((right * here[None]).reshape(depth, 2 * channels))
            result = jnp.dot(left, jnp.concatenate(columns, axis=1), preferred_element_type=jnp.float32)
            if not exact:
                result = result * scale
            result = result.astype(jnp.bfloat16)

            @pl.when(group > 0)
            def _():
                write(group - 1, pair).wait()

            for step in range(steps):
                one_step = result[step * channels : (step + 1) * channels]
                for part in range(4):
                    result_v[pair, step, part // 2, part % 2] = one_step[:, part * channels : (part + 1) * channels]
            write(group, pair).start()
        return carry

    groups = bins // ROWS
    lax.fori_loop(0, groups, stack_group, 0)
    for pair in range(pairs):
        write(groups - 1, pair).wait()


def shards(strain, kernel, plan):
    fibres, wins = lax.axis_size("fibre"), lax.axis_size("win")
    channels, own_windows, samples = strain.shape
    margin, half_time = kernel.shape[0] // 2, kernel.shape[1] // 2
    bins = FB // wins
    halo = -(-margin // ROWS) * ROWS
    assert own_windows == 1 and bins % BLK == 0 and fibres & (fibres - 1) == 0
    table = transform_table(samples, bins, half_time)
    phases = phase_table(samples, half_time)
    any_space = pl.BlockSpec(memory_space=pl.ANY)
    gathered = pl.pallas_call(
        functools.partial(spectra_kernel, fibres, wins, margin, half_time),
        out_shape=jax.ShapeDtypeStruct((fibres, wins, 2, bins, channels), jnp.bfloat16),
        in_specs=[
            pl.BlockSpec(memory_space=pltpu.SMEM),
            pl.BlockSpec(memory_space=pltpu.HBM),
            pl.BlockSpec(memory_space=pltpu.HBM),
            pl.BlockSpec(memory_space=pltpu.HBM),
        ],
        out_specs=any_space,
        scratch_shapes=[
            pltpu.VMEM(phases.shape, jnp.float32),
            pltpu.VMEM(table.shape, jnp.bfloat16),
            pltpu.VMEM((channels + 2 * halo, samples), jnp.bfloat16),
            pltpu.VMEM((samples, channels + 2 * halo), jnp.bfloat16),
            pltpu.VMEM((channels + 2 * halo, kernel.shape[1] * channels), jnp.bfloat16),
            pltpu.VMEM((wins, 2, bins, channels), jnp.bfloat16),
            pltpu.VMEM((fibres, wins, 2, bins, channels), jnp.bfloat16),
            pltpu.SemaphoreType.DMA((3,)),
            pltpu.SemaphoreType.DMA((2,)),
            pltpu.SemaphoreType.DMA((2,)),
            pltpu.SemaphoreType.DMA((wins,)),
            pltpu.SemaphoreType.DMA((wins,)),
            pltpu.SemaphoreType.DMA,
            pltpu.SemaphoreType.DMA((fibres, wins)),
            pltpu.SemaphoreType.DMA((fibres, wins)),
        ],
        compiler_params=pltpu.CompilerParams(
            collective_id=0, has_side_effects=True, vmem_limit_bytes=60 * 1024 * 1024
        ),
        name="spectra",
    )(kernel.astype(jnp.float32), jnp.asarray(phases), jnp.asarray(table), strain.reshape(channels, samples))

    steps = plan.shape[0]
    return pl.pallas_call(
        functools.partial(stack_kernel, steps, 1.0 / math.sqrt(wins * own_windows)),
        out_shape=jax.ShapeDtypeStruct((steps, bins, 2, channels, channels), jnp.bfloat16),
        in_specs=[pl.BlockSpec(memory_space=pltpu.SMEM), any_space],
        out_specs=any_space,
        scratch_shapes=[
            pltpu.VMEM((steps + 1, wins, 2, bins, channels), jnp.bfloat16),
            pltpu.VMEM((steps * channels, wins * 2 * ROWS), jnp.bfloat16),
            pltpu.VMEM((wins * 2 * ROWS, 2 * channels), jnp.bfloat16),
            pltpu.VMEM((ROWS // 2, steps, 2, 2, channels, channels), jnp.bfloat16),
            pltpu.SemaphoreType.DMA((steps + 1,)),
            pltpu.SemaphoreType.DMA((ROWS // 2,)),
        ],
        compiler_params=pltpu.CompilerParams(vmem_limit_bytes=60 * 1024 * 1024),
        name="stacks",
    )(plan, gathered)


def solution(mesh):
    placed = (P("fibre", "win", None), P(), P())
    return jax.shard_map(
        shards,
        mesh=mesh,
        in_specs=placed,
        out_specs=P(None, "win", None, None, "fibre"),
        check_vma=False,
    )
```

```python
import functools
import math

import jax
import jax.numpy as jnp
import ml_dtypes
import numpy as np
from jax import lax
from jax.experimental import pallas as pl
from jax.experimental.pallas import tpu as pltpu
from jax.sharding import PartitionSpec as P

FB = 256
FLO = 8
BLK = 64
ROWS = 16
MESH = pl.DeviceIdType.MESH


def tap_order(half_time):
    order = [0]
    for offset in range(1, half_time + 1):
        order += [offset, -offset]
    return order


@functools.lru_cache(maxsize=None)
def transform_table(samples, bins, half_time):
    index = np.arange(samples, dtype=np.int64)
    picks = np.zeros((-(-2 * half_time // ROWS) * ROWS, samples), ml_dtypes.bfloat16)
    for row in range(half_time):
        picks[row, row] = 1
        picks[half_time + row, samples - half_time + row] = 1
    blocks = []
    for start in range(0, FB, bins):
        wanted = FLO + start + np.arange(bins, dtype=np.int64)
        angles = (wanted[:, None] * index[None, :] % samples) * (2.0 * np.pi / samples)
        exact = np.concatenate([np.cos(angles), -np.sin(angles)])
        high = exact.astype(ml_dtypes.bfloat16)
        low = (exact - high.astype(np.float64)).astype(ml_dtypes.bfloat16)
        blocks += [high, low, picks]
    return np.concatenate(blocks)


@functools.lru_cache(maxsize=None)
def phase_table(samples, half_time):
    wanted = FLO + np.arange(FB, dtype=np.int64)
    angles = wanted[:, None] * np.arange(1, half_time + 1)[None, :] % samples * (2.0 * np.pi / samples)
    return np.concatenate([np.cos(angles), np.sin(angles)], axis=1).astype(np.float32)


def gather_orders(count):
    bits = [1 << place for place in range(1, count.bit_length() - 1)]
    return [bits + [1], bits[::-1] + [1]]


def spectra_kernel(
    fibres, wins, margin, half_time,
    taps_hbm, phase_hbm, table_ref, strain_ref, out_ref,
    taps_ref, phase_ref, table_v, x_v, xt_v, band_v, white_v, held_v,
    load_sem, halo_send, halo_recv, swap_send, swap_recv, keep_sem, gather_send, gather_recv,
):
    me = lax.axis_index("fibre")
    win = lax.axis_index("win")
    channels = strain_ref.shape[0]
    bins = white_v.shape[2]
    halo = (x_v.shape[0] - channels) // 2
    chan_taps = 2 * margin + 1
    order = tap_order(half_time)

    load_table = pltpu.make_async_copy(table_ref, table_v, load_sem.at[0])
    load_table.start()
    load_own = pltpu.make_async_copy(strain_ref, x_v.at[pl.ds(0, channels)], load_sem.at[1])
    load_own.start()
    load_phase = pltpu.make_async_copy(phase_hbm, phase_ref, load_sem.at[2])
    load_phase.start()
    load_taps = pltpu.make_async_copy(taps_hbm, taps_ref, load_sem.at[3])
    load_taps.start()

    barrier = pltpu.get_barrier_semaphore()
    for step in range(1, fibres):
        pl.semaphore_signal(barrier, inc=1, device_id={"fibre": lax.rem(me + step, fibres)}, device_id_type=MESH)
    for step in range(1, wins):
        pl.semaphore_signal(barrier, inc=1, device_id={"win": lax.rem(win + step, wins)}, device_id_type=MESH)
    pl.semaphore_wait(barrier, fibres + wins - 2)

    to_right = pltpu.make_async_remote_copy(
        src_ref=strain_ref.at[pl.ds(channels - halo, halo)], dst_ref=x_v.at[pl.ds(channels, halo)],
        send_sem=halo_send.at[0], recv_sem=halo_recv.at[0],
        device_id={"fibre": lax.rem(me + 1, fibres)}, device_id_type=MESH,
    )
    to_left = pltpu.make_async_remote_copy(
        src_ref=strain_ref.at[pl.ds(0, halo)], dst_ref=x_v.at[pl.ds(channels + halo, halo)],
        send_sem=halo_send.at[1], recv_sem=halo_recv.at[1],
        device_id={"fibre": lax.rem(me + fibres - 1, fibres)}, device_id_type=MESH,
    )
    first, last = me == 0, me == fibres - 1

    @pl.when(jnp.logical_not(last))
    def _():
        to_right.start()

    @pl.when(jnp.logical_not(first))
    def _():
        to_left.start()

    @pl.when(first)
    def _():
        x_v[channels : channels + halo, :] = jnp.zeros((halo, x_v.shape[1]), x_v.dtype)

    @pl.when(last)
    def _():
        x_v[channels + halo :, :] = jnp.zeros((halo, x_v.shape[1]), x_v.dtype)

    load_own.wait()

    def turn_over(piece, carry):
        columns = pl.ds(pl.multiple_of(piece * 256, 256), 256)
        xt_v[columns, :channels] = x_v[:channels, columns].astype(jnp.float32).T.astype(jnp.bfloat16)
        return carry

    lax.fori_loop(0, x_v.shape[1] // 256, turn_over, 0)

    load_taps.wait()

    def band_rows(first_row, rows, source):
        lag = source - lax.broadcasted_iota(jnp.int32, (rows, channels), 1) + margin
        totals = [jnp.zeros((rows, channels), jnp.float32)] * len(order)
        for tap in range(chan_taps):
            here = lag == tap
            totals = [
                jnp.where(here, taps_ref[tap, offset + half_time], total) for total, offset in zip(totals, order)
            ]
        for place, total in enumerate(totals):
            band_v[pl.ds(first_row, rows), place * channels : (place + 1) * channels] = total.astype(jnp.bfloat16)

    def own_rows(piece, carry):
        first_row = pl.multiple_of(piece * 2 * ROWS, 2 * ROWS)
        band_rows(first_row, 2 * ROWS, lax.broadcasted_iota(jnp.int32, (2 * ROWS, channels), 0) + first_row)
        return carry

    lax.fori_loop(0, channels // (2 * ROWS), own_rows, 0)
    row = lax.broadcasted_iota(jnp.int32, (2 * halo, channels), 0)
    band_rows(channels, 2 * halo, row - halo + jnp.where(row < halo, 0, channels))

    @pl.when(jnp.logical_not(last))
    def _():
        to_right.wait_send()
        to_left.wait_recv()

    @pl.when(jnp.logical_not(first))
    def _():
        to_left.wait_send()
        to_right.wait_recv()

    xt_v[:, channels:] = x_v[channels:, :].astype(jnp.float32).T.astype(jnp.bfloat16)
    load_table.wait()
    load_phase.wait()
    group_rows = table_v.shape[0] // wins

    def whiten_group(group, into):
        base = pl.multiple_of(group * group_rows, ROWS)
        spectra = jnp.dot(
            table_v[pl.ds(base, group_rows), :], xt_v[...], preferred_element_type=jnp.float32
        )
        both = spectra[: 2 * bins] + spectra[2 * bins : 4 * bins]
        high = both.astype(jnp.bfloat16)
        low = (both - high.astype(jnp.float32)).astype(jnp.bfloat16)
        edges = spectra[4 * bins :].astype(jnp.bfloat16)
        parts = jnp.dot(
            jnp.concatenate([high, low, edges]), band_v[...], preferred_element_type=jnp.float32
        )
        tails = parts[4 * bins :]

        def tail(row, offset):
            place = order.index(offset)
            return tails[row : row + 1, place * channels : (place + 1) * channels]

        before = {m: sum(tail(u, m + u) for u in range(half_time - m + 1)) for m in range(1, half_time + 1)}
        after = {
            m: sum(tail(2 * half_time - v, -(v + m)) for v in range(1, half_time - m + 1)) for m in range(half_time)
        }
        shifted = parts[: 2 * bins] + parts[2 * bins : 4 * bins]
        real = shifted[:bins, :channels] - after[0]
        imag = shifted[bins:, :channels]
        bin_rows = pl.ds(pl.multiple_of(group * bins, bins), bins)
        for offset in range(1, half_time + 1):
            pair = shifted[:, (2 * offset - 1) * channels : (2 * offset + 1) * channels]
            ahead_re = pair[:bins, :channels] - before[offset]
            back_re = pair[:bins, channels:]
            if offset in after:
                back_re = back_re - after[offset]
            ahead_im, back_im = pair[bins:, :channels], pair[bins:, channels:]
            cos = phase_ref[bin_rows, offset - 1 : offset]
            sin = phase_ref[bin_rows, half_time + offset - 1 : half_time + offset]
            real += cos * (ahead_re + back_re) - sin * (ahead_im - back_im)
            imag += cos * (ahead_im + back_im) + sin * (ahead_re - back_re)
        magnitude = jnp.sqrt(real * real + imag * imag)
        for start in range(0, bins, BLK):
            level = jnp.mean(magnitude[start : start + BLK], axis=0, keepdims=True) + 1e-06
            factor = 1.0 / level
            into[0, start : start + BLK] = (real[start : start + BLK] * factor).astype(jnp.bfloat16)
            into[1, start : start + BLK] = (imag[start : start + BLK] * factor).astype(jnp.bfloat16)

    def swap(step):
        target = lax.bitwise_xor(win, step)
        return pltpu.make_async_remote_copy(
            src_ref=white_v.at[target], dst_ref=held_v.at[me, win],
            send_sem=swap_send.at[step], recv_sem=swap_recv.at[step],
            device_id={"win": target}, device_id_type=MESH,
        )

    def swap_arrival(step):
        source = lax.bitwise_xor(win, step)
        return pltpu.make_async_remote_copy(
            src_ref=white_v.at[win], dst_ref=held_v.at[me, source],
            send_sem=swap_send.at[step], recv_sem=swap_recv.at[step],
            device_id={"win": source}, device_id_type=MESH,
        )

    orders = gather_orders(fibres)

    def hop(step, away, bit):
        block = lax.bitwise_xor(me, away)
        window = lax.bitwise_xor(win, step)
        return pltpu.make_async_remote_copy(
            src_ref=held_v.at[block, window], dst_ref=held_v.at[block, window],
            send_sem=gather_send.at[away ^ bit, step], recv_sem=gather_recv.at[away ^ bit, step],
            device_id={"fibre": lax.bitwise_xor(me, bit)}, device_id_type=MESH,
        )

    started = []

    turns = [0] + list(range(wins - 1, 0, -1))

    def route(step, away):
        place = turns.index(step)
        if place < wins // 2:
            line = orders[place % 2]
            latest = max([spot for spot, bit in enumerate(line) if away & bit], default=-1)
            return (line[latest] if away else 0), line[latest + 1 :]
        if away & 1:
            return 1, []
        return away, ([] if away else list(range(2, fibres, 2))) + [1]

    def depth(step, away):
        count = 0
        while away:
            away ^= route(step, away)[0]
            count += 1
        return count

    def settle(step, away):
        came, onward = route(step, away)
        if came:
            hop(step, away ^ came, came).wait_recv()
        elif step:
            swap_arrival(step).wait_recv()
        for bit in onward:
            copy = hop(step, away, bit)
            copy.start()
            started.append(copy)
        block, window = lax.bitwise_xor(me, away), lax.bitwise_xor(win, step)
        pltpu.make_async_copy(held_v.at[block, window], out_ref.at[block, window], keep_sem).start()

    events = sorted(
        (place + depth(step, away), place, depth(step, away & ~1), away, step)
        for place, step in enumerate(turns) for away in range(fibres)
    )
    for turn, step in enumerate(turns):
        if step:
            target = lax.bitwise_xor(win, step)
            whiten_group(target, white_v.at[target])
            swap(step).start()
        else:
            whiten_group(win, held_v.at[me, win])
        due = [event for event in events if event[0] + (2 if event[1] else 1 if event[3] else 0) <= turn]
        events = [event for event in events if event not in due]
        for _, _, _, away, due_step in due:
            settle(due_step, away)
    for _, _, _, away, step in events:
        settle(step, away)
    for step in range(1, wins):
        swap(step).wait_send()
    for copy in started:
        copy.wait_send()
    pltpu.make_async_copy(held_v, out_ref, keep_sem).wait()


def stack_kernel(steps, scale, per_turn, plan_ref, gathered_ref, out_ref, blocks_v, left_v, right_v, result_v, load_sem, out_sem):
    wins, _, bins, channels = gathered_ref.shape[1:]
    depth = wins * 2 * ROWS
    exact = math.frexp(scale)[0] == 0.5
    loads = []
    for place in range(steps + 1):
        block = plan_ref[place] if place < steps else lax.axis_index("fibre")
        loads.append(pltpu.make_async_copy(gathered_ref.at[block], blocks_v.at[place], load_sem.at[place]))
        loads[-1].start()
    for load in loads:
        load.wait()
    row = lax.broadcasted_iota(jnp.int32, (ROWS, 2 * channels), 0)

    def write(turn, step):
        slot = lax.rem(turn, 2)
        return pltpu.make_async_copy(
            result_v.at[slot, step], out_ref.at[step, pl.ds(turn * per_turn, per_turn)], out_sem.at[slot, step]
        )

    def stack_turn(turn, carry):
        slot = lax.rem(turn, 2)
        first_bin = turn * per_turn

        @pl.when(lax.rem(first_bin, ROWS) == 0)
        def _():
            group = pl.ds(pl.multiple_of(first_bin, ROWS), ROWS)
            for step in range(steps):
                piece = blocks_v[step, :, :, group, :].reshape(depth, channels).astype(jnp.float32)
                if exact:
                    piece = piece * scale
                left_v[step * channels : (step + 1) * channels, :] = piece.T.astype(jnp.bfloat16)
            real = blocks_v[steps, :, 0, group, :]
            imag = blocks_v[steps, :, 1, group, :]
            right_v[:, :channels] = jnp.stack([real, imag], axis=1).reshape(depth, channels)
            right_v[:, channels:] = jnp.stack([imag, -real], axis=1).reshape(depth, channels)

        @pl.when(turn >= 2)
        def _():
            for step in range(steps):
                write(turn - 2, step).wait()

        right = right_v[...].reshape(wins * 2, ROWS, 2 * channels)
        left = left_v[...]
        for pair in range(0, per_turn, 2):
            columns = []
            for place in (pair, pair + 1):
                here = jnp.where(row == lax.rem(first_bin + place, ROWS), 1.0, 0.0).astype(jnp.bfloat16)
                columns.append((right * here[None]).reshape(depth, 2 * channels))
            result = jnp.dot(left, jnp.concatenate(columns, axis=1), preferred_element_type=jnp.float32)
            if not exact:
                result = result * scale
            result = result.astype(jnp.bfloat16)
            for step in range(steps):
                rows = result[step * channels : (step + 1) * channels]
                for part in range(4):
                    result_v[slot, step, pair + part // 2, part % 2] = rows[:, part * channels : (part + 1) * channels]
        for step in range(steps):
            write(turn, step).start()
        return carry

    turns = bins // per_turn
    lax.fori_loop(0, turns, stack_turn, 0)
    for turn in (turns - 2, turns - 1):
        for step in range(steps):
            write(turn, step).wait()


def shards(strain, kernel, plan):
    fibres, wins = lax.axis_size("fibre"), lax.axis_size("win")
    channels, own_windows, samples = strain.shape
    margin, half_time = kernel.shape[0] // 2, kernel.shape[1] // 2
    bins = FB // wins
    halo = -(-margin // ROWS) * ROWS
    assert own_windows == 1 and bins % BLK == 0 and fibres & (fibres - 1) == 0 and wins & (wins - 1) == 0
    table = transform_table(samples, bins, half_time)
    phases = phase_table(samples, half_time)
    any_space = pl.BlockSpec(memory_space=pl.ANY)
    gathered = pl.pallas_call(
        functools.partial(spectra_kernel, fibres, wins, margin, half_time),
        out_shape=jax.ShapeDtypeStruct((fibres, wins, 2, bins, channels), jnp.bfloat16),
        in_specs=[
            pl.BlockSpec(memory_space=pltpu.HBM),
            pl.BlockSpec(memory_space=pltpu.HBM),
            pl.BlockSpec(memory_space=pltpu.HBM),
            pl.BlockSpec(memory_space=pltpu.HBM),
        ],
        out_specs=any_space,
        scratch_shapes=[
            pltpu.SMEM(kernel.shape, jnp.float32),
            pltpu.VMEM(phases.shape, jnp.float32),
            pltpu.VMEM(table.shape, jnp.bfloat16),
            pltpu.VMEM((channels + 2 * halo, samples), jnp.bfloat16),
            pltpu.VMEM((samples, channels + 2 * halo), jnp.bfloat16),
            pltpu.VMEM((channels + 2 * halo, kernel.shape[1] * channels), jnp.bfloat16),
            pltpu.VMEM((wins, 2, bins, channels), jnp.bfloat16),
            pltpu.VMEM((fibres, wins, 2, bins, channels), jnp.bfloat16),
            pltpu.SemaphoreType.DMA((4,)),
            pltpu.SemaphoreType.DMA((2,)),
            pltpu.SemaphoreType.DMA((2,)),
            pltpu.SemaphoreType.DMA((wins,)),
            pltpu.SemaphoreType.DMA((wins,)),
            pltpu.SemaphoreType.DMA,
            pltpu.SemaphoreType.DMA((fibres, wins)),
            pltpu.SemaphoreType.DMA((fibres, wins)),
        ],
        compiler_params=pltpu.CompilerParams(
            collective_id=0, has_side_effects=True, vmem_limit_bytes=60 * 1024 * 1024
        ),
        name="spectra",
    )(kernel.astype(jnp.float32), jnp.asarray(phases), jnp.asarray(table), strain.reshape(channels, samples))

    steps = plan.shape[0]
    per_turn = 8
    return pl.pallas_call(
        functools.partial(stack_kernel, steps, 1.0 / math.sqrt(wins * own_windows), per_turn),
        out_shape=jax.ShapeDtypeStruct((steps, bins, 2, channels, channels), jnp.bfloat16),
        in_specs=[pl.BlockSpec(memory_space=pltpu.SMEM), any_space],
        out_specs=any_space,
        scratch_shapes=[
            pltpu.VMEM((steps + 1, wins, 2, bins, channels), jnp.bfloat16),
            pltpu.VMEM((steps * channels, wins * 2 * ROWS), jnp.bfloat16),
            pltpu.VMEM((wins * 2 * ROWS, 2 * channels), jnp.bfloat16),
            pltpu.VMEM((2, steps, per_turn, 2, channels, channels), jnp.bfloat16),
            pltpu.SemaphoreType.DMA((steps + 1,)),
            pltpu.SemaphoreType.DMA((2, steps)),
        ],
        compiler_params=pltpu.CompilerParams(vmem_limit_bytes=60 * 1024 * 1024),
        name="stacks",
    )(plan, gathered)


def solution(mesh):
    placed = (P("fibre", "win", None), P(), P())
    return jax.shard_map(
        shards,
        mesh=mesh,
        in_specs=placed,
        out_specs=P(None, "win", None, None, "fibre"),
        check_vma=False,
    )
```

```python
import functools
import math

import jax
import jax.numpy as jnp
import ml_dtypes
import numpy as np
from jax import lax
from jax.experimental import pallas as pl
from jax.experimental.pallas import tpu as pltpu
from jax.sharding import PartitionSpec as P

FB = 256
FLO = 8
BLK = 64
ROWS = 16
MESH = pl.DeviceIdType.MESH


def tap_order(half_time):
    order = [0]
    for offset in range(1, half_time + 1):
        order += [offset, -offset]
    return order


@functools.lru_cache(maxsize=None)
def transform_table(samples, bins, half_time):
    index = np.arange(samples, dtype=np.int64)
    picks = np.zeros((-(-2 * half_time // ROWS) * ROWS, samples), ml_dtypes.bfloat16)
    for row in range(half_time):
        picks[row, row] = 1
        picks[half_time + row, samples - half_time + row] = 1
    blocks = []
    for start in range(0, FB, bins):
        wanted = FLO + start + np.arange(bins, dtype=np.int64)
        angles = (wanted[:, None] * index[None, :] % samples) * (2.0 * np.pi / samples)
        exact = np.concatenate([np.cos(angles), -np.sin(angles)])
        high = exact.astype(ml_dtypes.bfloat16)
        low = (exact - high.astype(np.float64)).astype(ml_dtypes.bfloat16)
        blocks += [high, low, picks]
    return np.concatenate(blocks)


@functools.lru_cache(maxsize=None)
def phase_table(samples, half_time):
    wanted = FLO + np.arange(FB, dtype=np.int64)
    angles = wanted[:, None] * np.arange(1, half_time + 1)[None, :] % samples * (2.0 * np.pi / samples)
    return np.concatenate([np.cos(angles), np.sin(angles)], axis=1).astype(np.float32)


def gather_orders(count):
    bits = [1 << place for place in range(1, count.bit_length() - 1)]
    return [bits + [1], bits[::-1] + [1]]


def spectra_kernel(
    fibres, wins, margin, half_time,
    taps_hbm, phase_hbm, table_ref, strain_ref, out_ref,
    taps_v, taps_ref, phase_ref, table_v, x_v, xt_v, band_v, white_v, held_v,
    load_sem, halo_send, halo_recv, swap_send, swap_recv, keep_sem, gather_send, gather_recv,
):
    me = lax.axis_index("fibre")
    win = lax.axis_index("win")
    channels = strain_ref.shape[0]
    bins = white_v.shape[2]
    halo = (x_v.shape[0] - channels) // 2
    chan_taps = 2 * margin + 1
    order = tap_order(half_time)

    load_table = pltpu.make_async_copy(table_ref, table_v, load_sem.at[0])
    load_table.start()
    load_own = pltpu.make_async_copy(strain_ref, x_v.at[pl.ds(0, channels)], load_sem.at[1])
    load_own.start()
    load_phase = pltpu.make_async_copy(phase_hbm, phase_ref, load_sem.at[2])
    load_phase.start()
    load_taps = pltpu.make_async_copy(taps_hbm, taps_v, load_sem.at[3])
    load_taps.start()

    barrier = pltpu.get_barrier_semaphore()
    for step in range(1, fibres):
        pl.semaphore_signal(barrier, inc=1, device_id={"fibre": lax.rem(me + step, fibres)}, device_id_type=MESH)
    for step in range(1, wins):
        pl.semaphore_signal(barrier, inc=1, device_id={"win": lax.rem(win + step, wins)}, device_id_type=MESH)
    pl.semaphore_wait(barrier, fibres + wins - 2)

    to_right = pltpu.make_async_remote_copy(
        src_ref=strain_ref.at[pl.ds(channels - halo, halo)], dst_ref=x_v.at[pl.ds(channels, halo)],
        send_sem=halo_send.at[0], recv_sem=halo_recv.at[0],
        device_id={"fibre": lax.rem(me + 1, fibres)}, device_id_type=MESH,
    )
    to_left = pltpu.make_async_remote_copy(
        src_ref=strain_ref.at[pl.ds(0, halo)], dst_ref=x_v.at[pl.ds(channels + halo, halo)],
        send_sem=halo_send.at[1], recv_sem=halo_recv.at[1],
        device_id={"fibre": lax.rem(me + fibres - 1, fibres)}, device_id_type=MESH,
    )
    first, last = me == 0, me == fibres - 1

    @pl.when(jnp.logical_not(last))
    def _():
        to_right.start()

    @pl.when(jnp.logical_not(first))
    def _():
        to_left.start()

    @pl.when(first)
    def _():
        x_v[channels : channels + halo, :] = jnp.zeros((halo, x_v.shape[1]), x_v.dtype)

    @pl.when(last)
    def _():
        x_v[channels + halo :, :] = jnp.zeros((halo, x_v.shape[1]), x_v.dtype)

    load_own.wait()

    def turn_over(piece, carry):
        columns = pl.ds(pl.multiple_of(piece * 256, 256), 256)
        xt_v[columns, :channels] = x_v[:channels, columns].astype(jnp.float32).T.astype(jnp.bfloat16)
        return carry

    lax.fori_loop(0, x_v.shape[1] // 256, turn_over, 0)

    load_taps.wait()
    taps_ref[...] = taps_v[...].astype(jnp.float32)

    def band_rows(first_row, rows, source):
        lag = source - lax.broadcasted_iota(jnp.int32, (rows, channels), 1) + margin
        totals = [jnp.zeros((rows, channels), jnp.float32)] * len(order)
        for tap in range(chan_taps):
            here = lag == tap
            totals = [
                jnp.where(here, taps_ref[offset + half_time : offset + half_time + 1, tap : tap + 1], total)
                for total, offset in zip(totals, order)
            ]
        for place, total in enumerate(totals):
            band_v[pl.ds(first_row, rows), place * channels : (place + 1) * channels] = total.astype(jnp.bfloat16)

    def own_rows(piece, carry):
        first_row = pl.multiple_of(piece * 2 * ROWS, 2 * ROWS)
        band_rows(first_row, 2 * ROWS, lax.broadcasted_iota(jnp.int32, (2 * ROWS, channels), 0) + first_row)
        return carry

    lax.fori_loop(0, channels // (2 * ROWS), own_rows, 0)
    row = lax.broadcasted_iota(jnp.int32, (2 * halo, channels), 0)
    band_rows(channels, 2 * halo, row - halo + jnp.where(row < halo, 0, channels))

    @pl.when(jnp.logical_not(last))
    def _():
        to_right.wait_send()
        to_left.wait_recv()

    @pl.when(jnp.logical_not(first))
    def _():
        to_left.wait_send()
        to_right.wait_recv()

    xt_v[:, channels:] = x_v[channels:, :].astype(jnp.float32).T.astype(jnp.bfloat16)
    load_table.wait()
    load_phase.wait()
    group_rows = table_v.shape[0] // wins

    def whiten_group(group, into):
        base = pl.multiple_of(group * group_rows, ROWS)
        spectra = jnp.dot(
            table_v[pl.ds(base, group_rows), :], xt_v[...], preferred_element_type=jnp.float32
        )
        both = spectra[: 2 * bins] + spectra[2 * bins : 4 * bins]
        high = both.astype(jnp.bfloat16)
        low = (both - high.astype(jnp.float32)).astype(jnp.bfloat16)
        edges = spectra[4 * bins :].astype(jnp.bfloat16)
        parts = jnp.dot(
            jnp.concatenate([high, low, edges]), band_v[...], preferred_element_type=jnp.float32
        )
        tails = parts[4 * bins :]

        def tail(row, offset):
            place = order.index(offset)
            return tails[row : row + 1, place * channels : (place + 1) * channels]

        before = {m: sum(tail(u, m + u) for u in range(half_time - m + 1)) for m in range(1, half_time + 1)}
        after = {
            m: sum(tail(2 * half_time - v, -(v + m)) for v in range(1, half_time - m + 1)) for m in range(half_time)
        }
        shifted = parts[: 2 * bins] + parts[2 * bins : 4 * bins]
        real = shifted[:bins, :channels] - after[0]
        imag = shifted[bins:, :channels]
        bin_rows = pl.ds(pl.multiple_of(group * bins, bins), bins)
        for offset in range(1, half_time + 1):
            pair = shifted[:, (2 * offset - 1) * channels : (2 * offset + 1) * channels]
            ahead_re = pair[:bins, :channels] - before[offset]
            back_re = pair[:bins, channels:]
            if offset in after:
                back_re = back_re - after[offset]
            ahead_im, back_im = pair[bins:, :channels], pair[bins:, channels:]
            cos = phase_ref[bin_rows, offset - 1 : offset]
            sin = phase_ref[bin_rows, half_time + offset - 1 : half_time + offset]
            real += cos * (ahead_re + back_re) - sin * (ahead_im - back_im)
            imag += cos * (ahead_im + back_im) + sin * (ahead_re - back_re)
        magnitude = jnp.sqrt(real * real + imag * imag)
        for start in range(0, bins, BLK):
            level = jnp.mean(magnitude[start : start + BLK], axis=0, keepdims=True) + 1e-06
            factor = 1.0 / level
            into[0, start : start + BLK] = (real[start : start + BLK] * factor).astype(jnp.bfloat16)
            into[1, start : start + BLK] = (imag[start : start + BLK] * factor).astype(jnp.bfloat16)

    def swap(step):
        target = lax.bitwise_xor(win, step)
        return pltpu.make_async_remote_copy(
            src_ref=white_v.at[target], dst_ref=held_v.at[me, win],
            send_sem=swap_send.at[step], recv_sem=swap_recv.at[step],
            device_id={"win": target}, device_id_type=MESH,
        )

    def swap_arrival(step):
        source = lax.bitwise_xor(win, step)
        return pltpu.make_async_remote_copy(
            src_ref=white_v.at[win], dst_ref=held_v.at[me, source],
            send_sem=swap_send.at[step], recv_sem=swap_recv.at[step],
            device_id={"win": source}, device_id_type=MESH,
        )

    orders = gather_orders(fibres)

    def hop(step, away, bit):
        block = lax.bitwise_xor(me, away)
        window = lax.bitwise_xor(win, step)
        return pltpu.make_async_remote_copy(
            src_ref=held_v.at[block, window], dst_ref=held_v.at[block, window],
            send_sem=gather_send.at[away ^ bit, step], recv_sem=gather_recv.at[away ^ bit, step],
            device_id={"fibre": lax.bitwise_xor(me, bit)}, device_id_type=MESH,
        )

    started = []

    turns = [0] + list(range(wins - 1, 0, -1))

    def route(step, away):
        place = turns.index(step)
        if place == 0:
            line = orders[place % 2]
            latest = max([spot for spot, bit in enumerate(line) if away & bit], default=-1)
            return (line[latest] if away else 0), line[latest + 1 :]
        if away & 1:
            return 1, []
        return away, ([] if away else list(range(2, fibres, 2))) + [1]

    def depth(step, away):
        count = 0
        while away:
            away ^= route(step, away)[0]
            count += 1
        return count

    def settle(step, away):
        came, onward = route(step, away)
        if came:
            hop(step, away ^ came, came).wait_recv()
        elif step:
            swap_arrival(step).wait_recv()
        for bit in onward:
            copy = hop(step, away, bit)
            copy.start()
            started.append(copy)
        block, window = lax.bitwise_xor(me, away), lax.bitwise_xor(win, step)
        pltpu.make_async_copy(held_v.at[block, window], out_ref.at[block, window], keep_sem).start()

    events = sorted(
        (place + depth(step, away), place, depth(step, away & ~1), away, step)
        for place, step in enumerate(turns) for away in range(fibres)
    )
    for turn, step in enumerate(turns):
        if step:
            target = lax.bitwise_xor(win, step)
            whiten_group(target, white_v.at[target])
            swap(step).start()
        else:
            whiten_group(win, held_v.at[me, win])
        due = [event for event in events if event[0] + (2 if event[1] else 1 if event[3] else 0) <= turn]
        events = [event for event in events if event not in due]
        for _, _, _, away, due_step in due:
            settle(due_step, away)
    for _, _, _, away, step in events:
        settle(step, away)
    for step in range(1, wins):
        swap(step).wait_send()
    for copy in started:
        copy.wait_send()
    pltpu.make_async_copy(held_v, out_ref, keep_sem).wait()


def stack_kernel(steps, scale, per_turn, plan_ref, gathered_ref, out_ref, blocks_v, left_v, right_v, result_v, load_sem, out_sem):
    wins, _, bins, channels = gathered_ref.shape[1:]
    depth = wins * 2 * ROWS
    exact = math.frexp(scale)[0] == 0.5
    loads = []
    for place in range(steps + 1):
        block = plan_ref[place] if place < steps else lax.axis_index("fibre")
        loads.append(pltpu.make_async_copy(gathered_ref.at[block], blocks_v.at[place], load_sem.at[place]))
        loads[-1].start()
    for load in loads:
        load.wait()
    row = lax.broadcasted_iota(jnp.int32, (ROWS, 2 * channels), 0)

    def write(turn, step):
        slot = lax.rem(turn, 2)
        return pltpu.make_async_copy(
            result_v.at[slot, step], out_ref.at[step, pl.ds(turn * per_turn, per_turn)], out_sem.at[slot, step]
        )

    def stack_turn(turn, carry):
        slot = lax.rem(turn, 2)
        first_bin = turn * per_turn

        @pl.when(lax.rem(first_bin, ROWS) == 0)
        def _():
            group = pl.ds(pl.multiple_of(first_bin, ROWS), ROWS)
            for step in range(steps):
                piece = blocks_v[step, :, :, group, :].reshape(depth, channels).astype(jnp.float32)
                if exact:
                    piece = piece * scale
                left_v[step * channels : (step + 1) * channels, :] = piece.T.astype(jnp.bfloat16)
            real = blocks_v[steps, :, 0, group, :]
            imag = blocks_v[steps, :, 1, group, :]
            right_v[:, :channels] = jnp.stack([real, imag], axis=1).reshape(depth, channels)
            right_v[:, channels:] = jnp.stack([imag, -real], axis=1).reshape(depth, channels)

        @pl.when(turn >= 2)
        def _():
            for step in range(steps):
                write(turn - 2, step).wait()

        right = right_v[...].reshape(wins * 2, ROWS, 2 * channels)
        left = left_v[...]
        for pair in range(0, per_turn, 2):
            columns = []
            for place in (pair, pair + 1):
                here = jnp.where(row == lax.rem(first_bin + place, ROWS), 1.0, 0.0).astype(jnp.bfloat16)
                columns.append((right * here[None]).reshape(depth, 2 * channels))
            result = jnp.dot(left, jnp.concatenate(columns, axis=1), preferred_element_type=jnp.float32)
            if not exact:
                result = result * scale
            result = result.astype(jnp.bfloat16)
            for step in range(steps):
                rows = result[step * channels : (step + 1) * channels]
                for part in range(4):
                    result_v[slot, step, pair + part // 2, part % 2] = rows[:, part * channels : (part + 1) * channels]
        for step in range(steps):
            write(turn, step).start()
        return carry

    turns = bins // per_turn
    lax.fori_loop(0, turns, stack_turn, 0)
    for turn in (turns - 2, turns - 1):
        for step in range(steps):
            write(turn, step).wait()


def shards(strain, kernel, plan):
    fibres, wins = lax.axis_size("fibre"), lax.axis_size("win")
    channels, own_windows, samples = strain.shape
    margin, half_time = kernel.shape[0] // 2, kernel.shape[1] // 2
    bins = FB // wins
    halo = -(-margin // ROWS) * ROWS
    assert own_windows == 1 and bins % BLK == 0 and fibres & (fibres - 1) == 0 and wins & (wins - 1) == 0
    table = transform_table(samples, bins, half_time)
    phases = phase_table(samples, half_time)
    any_space = pl.BlockSpec(memory_space=pl.ANY)
    gathered = pl.pallas_call(
        functools.partial(spectra_kernel, fibres, wins, margin, half_time),
        out_shape=jax.ShapeDtypeStruct((fibres, wins, 2, bins, channels), jnp.bfloat16),
        in_specs=[
            pl.BlockSpec(memory_space=pltpu.HBM),
            pl.BlockSpec(memory_space=pltpu.HBM),
            pl.BlockSpec(memory_space=pltpu.HBM),
            pl.BlockSpec(memory_space=pltpu.HBM),
        ],
        out_specs=any_space,
        scratch_shapes=[
            pltpu.VMEM(kernel.shape[::-1], kernel.dtype),
            pltpu.VMEM(kernel.shape[::-1], jnp.float32),
            pltpu.VMEM(phases.shape, jnp.float32),
            pltpu.VMEM(table.shape, jnp.bfloat16),
            pltpu.VMEM((channels + 2 * halo, samples), jnp.bfloat16),
            pltpu.VMEM((samples, channels + 2 * halo), jnp.bfloat16),
            pltpu.VMEM((channels + 2 * halo, kernel.shape[1] * channels), jnp.bfloat16),
            pltpu.VMEM((wins, 2, bins, channels), jnp.bfloat16),
            pltpu.VMEM((fibres, wins, 2, bins, channels), jnp.bfloat16),
            pltpu.SemaphoreType.DMA((4,)),
            pltpu.SemaphoreType.DMA((2,)),
            pltpu.SemaphoreType.DMA((2,)),
            pltpu.SemaphoreType.DMA((wins,)),
            pltpu.SemaphoreType.DMA((wins,)),
            pltpu.SemaphoreType.DMA,
            pltpu.SemaphoreType.DMA((fibres, wins)),
            pltpu.SemaphoreType.DMA((fibres, wins)),
        ],
        compiler_params=pltpu.CompilerParams(
            collective_id=0, has_side_effects=True, vmem_limit_bytes=60 * 1024 * 1024
        ),
        name="spectra",
    )(kernel.T, jnp.asarray(phases), jnp.asarray(table), strain.reshape(channels, samples))

    steps = plan.shape[0]
    per_turn = 8
    return pl.pallas_call(
        functools.partial(stack_kernel, steps, 1.0 / math.sqrt(wins * own_windows), per_turn),
        out_shape=jax.ShapeDtypeStruct((steps, bins, 2, channels, channels), jnp.bfloat16),
        in_specs=[pl.BlockSpec(memory_space=pltpu.SMEM), any_space],
        out_specs=any_space,
        scratch_shapes=[
            pltpu.VMEM((steps + 1, wins, 2, bins, channels), jnp.bfloat16),
            pltpu.VMEM((steps * channels, wins * 2 * ROWS), jnp.bfloat16),
            pltpu.VMEM((wins * 2 * ROWS, 2 * channels), jnp.bfloat16),
            pltpu.VMEM((2, steps, per_turn, 2, channels, channels), jnp.bfloat16),
            pltpu.SemaphoreType.DMA((steps + 1,)),
            pltpu.SemaphoreType.DMA((2, steps)),
        ],
        compiler_params=pltpu.CompilerParams(vmem_limit_bytes=60 * 1024 * 1024),
        name="stacks",
    )(plan, gathered)


def solution(mesh):
    placed = (P("fibre", "win", None), P(), P())
    return jax.shard_map(
        shards,
        mesh=mesh,
        in_specs=placed,
        out_specs=P(None, "win", None, None, "fibre"),
        check_vma=False,
    )
```
